128 devices in a mesh: row: 32 (over x_lo, z, y), col: 4 (over x_hi, core).
Axes of the slice: x: 4 (x_hi: 2, x_lo: 2; x = x_hi * 2 + x_lo), y: 4, z: 4, core: 2. Of those that a mesh axis runs over, the one named last changes fastest.
Arguments:
- spectra: bfloat16 [2, 20, 32, 4096], P(None, None, None, ('col', 'row')), may hold values from -6 to 6
Outputs:
- lag_partials: float32 [32, 4096, 4096], P(None, 'row', 'col')
The draws below stay inside these ranges and needn't reach their ends.
All inputs are finite; a program needn't handle non-finite values.
Results may differ from the reference program's by a relative error of at most 0.0029.
Values may be sent and summed in bfloat16 or wider, within the bound.
A program may use at most 256 MiB of HBM per device.

```python
import math
import jax
import jax.numpy as jnp
from jax import lax

C = 4096
F = 32
W = 20
N_ROW = 32


def levels(rng, dims, split, low, largest):
    def one(dim, parts):
        heights = jax.random.uniform(jax.random.fold_in(jax.random.fold_in(rng, 6), dim), (parts,), jnp.float32, low / len(split), largest / len(split))
        return jnp.repeat(jnp.exp(heights), dims[dim] // parts).reshape((-1,) + (1,) * (len(dims) - dim - 1))

    level = one(*split[0])
    for cut in split[1:]:
        level = level * one(*cut)
    return level


def normal_values(key, shape, deviation, most, split=(), kind=jnp.bfloat16):
    values = deviation * jax.random.normal(key, shape, jnp.float32)
    if split:
        values = values * levels(key, shape, split, -0.22, 0.18)
    return jnp.clip(values, -most, most).astype(kind)


def setup_inputs(seed: int = 0) -> dict:
    seeds = jax.random.split(jax.random.key(seed), 2)
    spectra = normal_values(seeds[0], (2, W, F, C), 1.0, 6.0, ((3, 128),))
    return dict(spectra=spectra)


def twiddle(block):
    nfreq = block.shape[2]
    nwin = block.shape[1]
    count = block.shape[3]
    scale = 1.0 / math.sqrt(2.0 * nwin * nfreq)
    lag_index = jnp.arange(nfreq, dtype=jnp.int32)[:, None]
    freq_index = jnp.arange(nfreq, dtype=jnp.int32)[None, :]
    phase = (lag_index * freq_index % nfreq).astype(jnp.float32) * (2.0 * math.pi / nfreq)
    cosine = jnp.cos(phase)[:, None, :, None]
    sine = jnp.sin(phase)[:, None, :, None]
    real_part = block[0].astype(jnp.float32)[None]
    imag_part = block[1].astype(jnp.float32)[None]
    first = scale * (real_part * cosine + imag_part * sine)
    second = scale * (imag_part * cosine - real_part * sine)
    stacked = jnp.stack([first, second], axis=1)
    stacked = jnp.transpose(stacked, (0, 4, 1, 2, 3)).reshape(nfreq, count, 2 * nwin * nfreq)
    return stacked.astype(jnp.bfloat16)

def reference(spectra):
    depth = 2 * W * F
    row_size = C // N_ROW
    right = spectra.reshape(depth, C).astype(jnp.float32)

    def step(group, accum):
        start = (group * row_size).astype(jnp.int32)
        block = lax.dynamic_slice_in_dim(spectra, start, row_size, 3)
        left = twiddle(block).astype(jnp.float32)
        partial_block = jnp.einsum('lik,kj->lij', left, right, precision=lax.Precision.HIGHEST)
        zero = jnp.zeros((), jnp.int32)
        return lax.dynamic_update_slice(accum, partial_block, (zero, start, zero))
    initial = jnp.zeros((F, C, C), jnp.float32)
    return lax.fori_loop(0, N_ROW, step, initial)
```

```python
import functools
import math

import jax
import jax.numpy as jnp
import numpy as np
from jax import lax
from jax.experimental import pallas as pl
from jax.experimental.pallas import tpu as pltpu
from jax.sharding import PartitionSpec as P

NW, NF, NC, NR = 20, 32, 32, 32
DEPTH = 2 * NW * NF
LANE = 128
SCALE = 1.0 / math.sqrt(float(DEPTH))

PIECES = 2
PLAN = (
    (0, 0, 0), (1, 1, 0), (2, 1, 0), (3, 1, 0), (4, 1, 0), (0, 1, 0), (1, 0, 0), (2, 0, 0),
    (3, 0, 0), (4, 0, 0), (0, 1, 1), (1, 0, 16), (2, 1, 3), (3, 1, 1), (4, 1, 12), (0, 1, 3),
    (1, 1, 12), (2, 0, 4), (3, 1, 16), (4, 0, 3), (0, 0, 3), (1, 0, 12), (2, 1, 12), (3, 0, 16),
    (4, 0, 12), (0, 1, 8), (1, 1, 8), (2, 0, 3), (3, 1, 3), (4, 0, 17), (0, 1, 12), (1, 1, 17),
    (2, 1, 8), (3, 1, 19), (4, 1, 2), (0, 1, 13), (1, 0, 8), (2, 0, 7), (3, 1, 2), (4, 0, 19),
    (0, 0, 2), (1, 0, 13), (2, 0, 29), (3, 0, 7), (4, 0, 29), (0, 1, 5), (1, 0, 29), (2, 1, 23),
    (3, 0, 20), (4, 1, 19), (0, 1, 11), (1, 0, 20), (2, 0, 6), (3, 0, 19), (4, 1, 18), (0, 0, 6),
    (1, 0, 9), (3, 1, 6), (4, 0, 31), (1, 1, 24), (3, 1, 22), (4, 0, 30),
)
STEPS = ((1, 0, 0), (0, 0, 1), (0, 0, 3), (0, 1, 0), (0, 3, 0))


def split_offset(offset):
    return offset // 16, offset // 4 % 4, offset % 4


def shifted(offset, step):
    x, z, y = split_offset(offset)
    return (x + step[0]) % 2 * 16 + (z + step[1]) % 4 * 4 + (y + step[2]) % 4


CLASSES = ((0, 16, 8, 24),) + tuple((r, r + 16, 16 - r, 32 - r) for r in range(1, 8))


def lane_tables():
    cosine = np.zeros(DEPTH)
    sine = np.zeros(DEPTH)
    sign = np.zeros(DEPTH)
    for c, bins in enumerate(CLASSES):
        for part in range(2):
            for q in range(4 * NW):
                if q < 64:
                    lane = c * LANE + part * 64 + q
                else:
                    lane = 8 * LANE + c // 4 * LANE + part * 64 + c % 4 * 16 + q - 64
                which = q // NW
                phase = 2.0 * math.pi * bins[which] / NF
                cosine[lane] = SCALE * math.cos(phase)
                sine[lane] = SCALE * math.sin(phase) * (1.0 if part == 0 else -1.0)
                sign[lane] = (1.0 if which < 2 else -1.0) * (-1.0 if part == 0 else 1.0)
    table = np.zeros((8, DEPTH), np.float32)
    table[0], table[1], table[2] = cosine, sine, sign
    return table


def gather_kernel(x_ref, all_ref, first_ref, flat, ordered, own, send_sem, recv_sem, first_send, first_recv, local_sem):
    row = lax.axis_index("row")
    col = lax.axis_index("col")
    x, z, y = row // 16, row // 4 % 4, row % 4
    far, core = col // 2, col % 2
    serves = core == z // 2
    crosses = far != x

    neighbours = []
    for step in STEPS:
        neighbours.append((x + step[0]) % 2 * 16 + (z + step[1]) % 4 * 4 + (y + step[2]) % 4)
    peer = far * 2 + 1 - core
    line = z % 2 * 16 + y * 4

    barrier = pltpu.get_barrier_semaphore()
    for neighbour in neighbours:
        pl.semaphore_signal(barrier, inc=1, device_id={"row": neighbour, "col": col})
    pl.semaphore_signal(barrier, inc=1, device_id={"row": row, "col": peer})

    @pl.when(jnp.logical_and(serves, crosses))
    def _():
        for i in range(4):
            pl.semaphore_signal(barrier, inc=1, device_id={"row": line + i, "col": x * 2 + core})

    flat[...] = x_ref[...].reshape(DEPTH, NC).astype(jnp.float32)
    for c, bins in enumerate(CLASSES):
        tail = 8 * LANE + c // 4 * LANE + c % 4 * 16
        for part in range(2):
            for i, f in enumerate(bins):
                start = part * NW * NF + f
                place = c * LANE + part * 64 + i * NW
                if i < 3:
                    ordered[pl.ds(place, NW), :] = flat[pl.ds(start, NW, stride=NF), :]
                else:
                    ordered[pl.ds(place, 4), :] = flat[pl.ds(start, 4, stride=NF), :]
                    ordered[pl.ds(tail + part * 64, 16), :] = flat[pl.ds(start + 4 * NF, 16, stride=NF), :]
    for t in range(10):
        own[:, t * LANE:(t + 1) * LANE] = ordered[t * LANE:(t + 1) * LANE, :].T.astype(jnp.bfloat16)

    pl.semaphore_wait(barrier, 7)

    keep = pltpu.make_async_copy(own, all_ref.at[row], local_sem)
    keep.start()
    target_row = far * 16 + (2 * core + x) * 4 + z
    to_first = pltpu.make_async_remote_copy(
        src_ref=own, dst_ref=first_ref.at[y], send_sem=first_send.at[0], recv_sem=first_recv.at[y],
        device_id={"row": target_row, "col": (1 - far) * 2 + core},
    )

    size = NC // PIECES

    def source(offset):
        ox, oz, oy = split_offset(offset)
        return (x - ox) % 2 * 16 + (z - oz) % 4 * 4 + (y - oy) % 4

    def receive(piece, offset):
        there = all_ref.at[source(offset), pl.ds(piece * size, size)]
        sem = recv_sem.at[piece * NR + offset]
        pltpu.make_async_copy(there, there, sem).wait()

    sent = []
    arrived = {(piece, 0) for piece in range(PIECES)}
    for n, (direction, piece, offset) in enumerate(PLAN):
        if (piece, offset) not in arrived:
            receive(piece, offset)
            arrived.add((piece, offset))
        rows = pl.ds(piece * size, size)
        place = all_ref.at[source(offset), rows]
        copy = pltpu.make_async_remote_copy(
            src_ref=own.at[rows] if offset == 0 else place,
            dst_ref=place,
            send_sem=send_sem.at[n],
            recv_sem=recv_sem.at[piece * NR + shifted(offset, STEPS[direction])],
            device_id={"row": neighbours[direction], "col": col},
        )
        copy.start()
        sent.append(copy)
        if n == 9:
            to_first.start()
    for direction, piece, offset in PLAN:
        place = (piece, shifted(offset, STEPS[direction]))
        if place not in arrived:
            receive(*place)
            arrived.add(place)
    keep.wait()

    def to_peer(src):
        return pltpu.make_async_remote_copy(
            src_ref=src, dst_ref=first_ref, send_sem=first_send.at[1], recv_sem=first_recv.at[4],
            device_id={"row": row, "col": peer},
        )

    @pl.when(serves)
    def _():
        @pl.when(crosses)
        def _():
            for i in range(4):
                pltpu.make_async_copy(first_ref.at[i], first_ref.at[i], first_recv.at[i]).wait()
            copy = to_peer(first_ref)
            copy.start()
            copy.wait_send()

        @pl.when(jnp.logical_not(crosses))
        def _():
            lines = all_ref.at[pl.ds(line, 4)]
            copy = to_peer(lines)
            copy.start()
            mine = pltpu.make_async_copy(lines, first_ref, local_sem)
            mine.start()
            mine.wait()
            copy.wait_send()

    @pl.when(jnp.logical_not(serves))
    def _():
        pltpu.make_async_copy(first_ref, first_ref, first_recv.at[4]).wait()

    to_first.wait_send()
    for copy in sent:
        copy.wait_send()


def butterflies(zero, eight, real, imag):
    c1, c2, c3 = (math.cos(math.pi * k / 8) for k in (1, 2, 3))
    e = [zero] + real + [eight]
    u0, u1, u2, u3, u4 = e[0] + e[8], e[1] + e[7], e[2] + e[6], e[3] + e[5], e[4]
    d0, d1, d2, d3 = e[0] - e[8], e[1] - e[7], e[2] - e[6], e[3] - e[5]
    v0, v1 = u0 + u4, u1 + u3
    w0, w1 = u0 - u4, c2 * (u1 - u3)
    g = c2 * d2
    h0, h1 = d0 + g, d0 - g
    p, q = c1 * d1 + c3 * d3, c3 * d1 - c1 * d3
    v2 = v0 + u2
    even = [v2 + v1, h0 + p, w0 + w1, h1 + q, v0 - u2, h1 - q, w0 - w1, h0 - p, v2 - v1]
    f = [None] + imag
    s1, s2, s3 = f[1] + f[7], f[2] + f[6], f[3] + f[5]
    t1, t2, t3 = f[1] - f[7], f[2] - f[6], f[3] - f[5]
    g = c2 * s2
    a, b = c3 * s1 + c1 * s3, c1 * s1 - c3 * s3
    g0, g1 = g + f[4], g - f[4]
    k = c2 * (t1 + t3)
    odd = [None, a + g0, k + t2, b + g1, t1 - t3, b - g1, k - t2, a - g0]
    out = [even[0]] + [even[m] - odd[m] for m in range(1, 8)] + [even[8]]
    return out + [even[m] + odd[m] for m in range(7, 0, -1)]


TILE = 256
BAND = 32


def product_kernel(table_ref, first_ref, all_ref, out_ref, left, prod, outs, sems):
    lane = lax.broadcasted_iota(jnp.int32, (LANE, LANE), 1) % 64

    def variants(t):
        span = slice(t * LANE, (t + 1) * LANE)
        value = first_ref[:, span].astype(jnp.float32)
        turned = pltpu.roll(value, 64, 1)
        one = value * table_ref[0:1, span] + turned * table_ref[1:2, span]
        sign = table_ref[2:3, span]
        plain = [value * SCALE, one]
        return plain, [turned * (sign * SCALE), pltpu.roll(one, 64, 1) * sign]

    tails = [variants(8), variants(9)]
    for c in range(8):
        plain, turned = variants(c)
        tail_plain, tail_turned = tails[c // 4]
        here = lane // 16 == c % 4
        for lag in range(2):
            if c == 0:
                real = [jnp.where(lane < 40, plain[lag], 0.0), jnp.zeros_like(plain[lag])]
                imag = [jnp.where(lane < 40, 0.0, plain[lag]), jnp.where(here, tail_plain[lag], 0.0)]
            else:
                real = [plain[lag], jnp.where(here, tail_plain[lag], 0.0)]
                imag = [turned[lag], jnp.where(here, tail_turned[lag], 0.0)]
            for kind, pair in enumerate((real, imag)):
                rows = slice((kind * 2 + lag) * LANE, (kind * 2 + lag + 1) * LANE)
                left[c, rows, :LANE] = pair[0].astype(jnp.bfloat16)
                left[c, rows, LANE:] = pair[1].astype(jnp.bfloat16)

    def writes(tile, band):
        slot = lax.rem(tile, 2)
        rows = pl.ds(band * BAND, BAND)
        return pltpu.make_async_copy(
            outs.at[slot, :, rows],
            out_ref.at[:, rows, pl.ds(pl.multiple_of(tile * TILE, TILE), TILE)],
            sems.at[slot, band],
        )

    bands = LANE // BAND
    tiles = out_ref.shape[2] // TILE

    @pl.loop(0, tiles)
    def _(tile):
        slot = lax.rem(tile, 2)
        rows = pl.ds(pl.multiple_of(tile * TILE, TILE), TILE)
        for c in range(8):
            right = jnp.concatenate(
                [all_ref[rows, c * LANE:(c + 1) * LANE], all_ref[rows, (8 + c // 4) * LANE:(9 + c // 4) * LANE]], axis=1
            )
            prod[c] = lax.dot_general(left[c], right, (((1,), (1,)), ((), ())), preferred_element_type=jnp.float32)

        @pl.loop(0, bands)
        def _(band):
            @pl.when(tile >= 2)
            def _():
                writes(tile - 2, band).wait()

            @pl.loop(0, BAND // 8)
            def _(block):
                start = pl.multiple_of(band * BAND + block * 8, 8)
                for lag in range(2):
                    real = [prod[c, pl.ds(lag * LANE + start, 8), :] for c in range(8)]
                    imag = [prod[c, pl.ds((2 + lag) * LANE + start, 8), :] for c in range(8)]
                    lags = butterflies(real[0], imag[0], real[1:], imag[1:])
                    for m in range(16):
                        outs[slot, lag + 2 * m, pl.ds(start, 8), :] = lags[m]

            writes(tile, band).start()

    for tile in range(max(tiles - 2, 0), tiles):
        for band in range(bands):
            writes(tile, band).wait()


def on_device(spectra):
    gathered, first = pl.pallas_call(
        gather_kernel,
        out_shape=(
            jax.ShapeDtypeStruct((NR, NC, DEPTH), jnp.bfloat16),
            jax.ShapeDtypeStruct((4, NC, DEPTH), jnp.bfloat16),
        ),
        in_specs=[pl.BlockSpec(memory_space=pltpu.VMEM)],
        out_specs=(pl.BlockSpec(memory_space=pl.ANY), pl.BlockSpec(memory_space=pl.ANY)),
        scratch_shapes=[
            pltpu.VMEM((DEPTH, NC), jnp.float32),
            pltpu.VMEM((DEPTH, NC), jnp.float32),
            pltpu.VMEM((NC, DEPTH), jnp.bfloat16),
            pltpu.SemaphoreType.DMA((len(PLAN),)),
            pltpu.SemaphoreType.DMA((PIECES * NR,)),
            pltpu.SemaphoreType.DMA((2,)),
            pltpu.SemaphoreType.DMA((5,)),
            pltpu.SemaphoreType.DMA,
        ],
        compiler_params=pltpu.CompilerParams(
            collective_id=0, has_side_effects=True, vmem_limit_bytes=16 * 1024 * 1024
        ),
        name="gather",
    )(spectra)
    table = jnp.asarray(lane_tables())
    return pl.pallas_call(
        product_kernel,
        out_shape=jax.ShapeDtypeStruct((NF, 4 * NC, NR * NC), jnp.float32),
        in_specs=[pl.BlockSpec(memory_space=pltpu.VMEM)] * 3,
        out_specs=pl.BlockSpec(memory_space=pl.ANY),
        scratch_shapes=[
            pltpu.VMEM((8, 4 * LANE, 2 * LANE), jnp.bfloat16),
            pltpu.VMEM((8, 4 * LANE, TILE), jnp.float32),
            pltpu.VMEM((2, NF, LANE, TILE), jnp.float32),
            pltpu.SemaphoreType.DMA((2, LANE // BAND)),
        ],
        compiler_params=pltpu.CompilerParams(vmem_limit_bytes=40 * 1024 * 1024),
        name="product",
    )(table, first.reshape(4 * NC, DEPTH), gathered.reshape(NR * NC, DEPTH))


def solution(mesh):
    return jax.shard_map(
        on_device,
        mesh=mesh,
        in_specs=(P(None, None, None, ("col", "row")),),
        out_specs=P(None, "row", "col"),
        check_vma=False,
    )
```

```python
import functools
import math

import jax
import jax.numpy as jnp
from jax import lax
from jax.experimental import pallas as pl
from jax.experimental.pallas import tpu as pltpu
from jax.sharding import PartitionSpec as P

NW, NF, NC, NR = 20, 32, 32, 32
DEPTH = 2 * NW * NF
LANE = 128
SCALE = 1.0 / math.sqrt(float(DEPTH))

PLAN_0 = (
    (2, 0, 0), (11, 1, 0), (3, 0, 0), (3, 1, 0), (4, 0, 0), (6, 0, 0), (6, 1, 0), (1, 1, 0),
    (2, 1, 0), (1, 0, 0), (4, 1, 0), (0, 1, 0), (0, 0, 0), (0, 0, 3), (2, 0, 3), (4, 0, 3),
    (3, 1, 3), (0, 1, 3), (4, 1, 28), (2, 1, 28), (1, 1, 28), (3, 1, 16), (0, 0, 5), (3, 0, 5),
    (4, 0, 12), (1, 1, 12), (2, 1, 12), (1, 1, 5), (10, 0, 5), (4, 0, 16), (2, 0, 4), (1, 1, 1),
    (10, 0, 3), (0, 0, 1), (4, 1, 12), (2, 0, 19), (4, 0, 19), (0, 1, 1), (4, 0, 15), (7, 1, 19),
    (3, 1, 7), (1, 1, 29), (4, 1, 29), (2, 1, 24), (-1, 0, 2), (0, 1, 7), (2, 1, 19), (1, 1, 13),
    (0, 0, 8), (1, 1, 20), (3, 0, 9), (4, 1, 13), (-1, 1, 4), (3, 1, 6), (2, 0, 15), (0, 0, 4),
    (1, 0, 25), (-1, 1, 15), (2, 0, 7), (4, 0, 18), (1, 0, 21), (-1, 1, 2), (-1, 1, 31), (-1, 0, 23),
    (3, 0, 25), (-1, 0, 17), (-1, 1, 8), (-1, 0, 28), (4, 0, 31), (2, 0, 11), (3, 1, 22), (-1, 1, 17),
    (-1, 1, 27), (-1, 1, 14), (-1, 1, 23), (-1, 1, 18), (-1, 1, 25), (-1, 1, 11), (-1, 1, 30), (-1, 0, 13),
    (-1, 1, 21), (-1, 0, 24), (-1, 0, 14), (-1, 1, 9), (-1, 0, 20), (-1, 0, 30), (-1, 0, 6), (-1, 1, 10),
    (-1, 0, 26), (-1, 0, 22), (-1, 0, 29), (-1, 0, 27), (-1, 0, 10), (-1, 1, 26),
)
PLAN_1 = (
    (3, 0, 0), (0, 1, 0), (5, 1, 0), (4, 0, 0), (1, 0, 0), (2, 0, 0), (4, 1, 0), (0, 0, 0),
    (2, 1, 0), (3, 1, 0), (1, 1, 0), (3, 0, 4), (0, 0, 4), (8, 1, 16), (1, 0, 4), (0, 0, 12),
    (4, 1, 16), (2, 0, 4), (1, 1, 16), (3, 1, 16), (0, 0, 1), (3, 1, 2), (8, 0, 12), (8, 0, 3),
    (1, 1, 4), (0, 1, 2), (3, 1, 3), (3, 1, 4), (-1, 0, 16), (1, 0, 8), (9, 0, 8), (1, 0, 5),
    (0, 0, 5), (4, 0, 28), (3, 1, 20), (1, 0, 28), (2, 0, 28), (0, 0, 7), (4, 1, 31), (1, 0, 17),
    (3, 1, 6), (4, 0, 3), (1, 1, 12), (4, 1, 2), (2, 1, 31), (0, 1, 5), (4, 1, 17), (3, 1, 7),
    (2, 0, 11), (3, 1, 18), (-1, 1, 28), (0, 0, 9), (4, 0, 1), (0, 1, 3), (-1, 0, 20), (2, 0, 27),
    (0, 1, 7), (1, 1, 24), (3, 0, 14), (-1, 0, 24), (2, 0, 31), (1, 1, 8), (0, 0, 6), (4, 0, 23),
    (-1, 1, 10), (-1, 0, 29), (2, 1, 27), (-1, 1, 1), (3, 1, 11), (-1, 1, 30), (-1, 1, 21), (-1, 0, 15),
    (-1, 0, 21), (-1, 0, 25), (-1, 1, 13), (-1, 0, 10), (-1, 1, 14), (-1, 0, 26), (-1, 1, 22), (-1, 1, 29),
    (-1, 0, 2), (-1, 0, 18), (-1, 1, 25), (-1, 1, 19), (-1, 0, 30), (-1, 1, 9), (-1, 1, 23), (-1, 0, 13),
    (-1, 1, 26), (-1, 0, 19), (-1, 1, 15), (-1, 0, 22),
)
PLANS = (PLAN_0, PLAN_1)
PIECES = 2
STEPS = (
    (1, 0, 0), (0, 0, 1), (0, 0, 3), (0, 1, 0), (0, 3, 0), (0, 0, 2), (0, 1, 1), (0, 1, 3),
    (0, 3, 3), (1, 0, 3), (1, 1, 0), (1, 3, 0),
)


def steps_of(plan):
    return sorted({STEPS[entry[0]] for entry in plan if entry[0] >= 0})


def split_offset(offset):
    return offset // 16, offset // 4 % 4, offset % 4


def shifted(offset, step):
    x, z, y = split_offset(offset)
    return (x + step[0]) % 2 * 16 + (z + step[1]) % 4 * 4 + (y + step[2]) % 4


CLASSES = ((0, 16, 8, 24),) + tuple((r, r + 16, 16 - r, 32 - r) for r in range(1, 8))


def gather_kernel(x_ref, all_ref, first_ref, flat, ordered, own, send_sem, recv_sem, first_send, first_recv, local_sem):
    row = lax.axis_index("row")
    col = lax.axis_index("col")
    x, z, y = row // 16, row // 4 % 4, row % 4
    far, core = col // 2, col % 2
    peer = {"row": row, "col": far * 2 + 1 - core}
    other = {"row": (1 - x) * 16 + row % 16, "col": (1 - far) * 2 + core}
    serves = core == z // 2
    passes = jnp.logical_and(serves, far != x)
    keeps = jnp.logical_and(serves, far == x)
    line = z % 2 * 4 + y
    size = NC // PIECES

    def there(step):
        return (x + step[0]) % 2 * 16 + (z + step[1]) % 4 * 4 + (y + step[2]) % 4

    def source(offset):
        ox, oz, oy = split_offset(offset)
        return (x - ox) % 2 * 16 + (z - oz) % 4 * 4 + (y - oy) % 4

    barrier = pltpu.get_barrier_semaphore()
    for which, plan in enumerate(PLANS):

        @pl.when(core == which)
        def _():
            for step in steps_of(plan):
                behind = ((-step[0]) % 2, (-step[1]) % 4, (-step[2]) % 4)
                pl.semaphore_signal(barrier, inc=1, device_id={"row": there(behind), "col": col})

    pl.semaphore_signal(barrier, inc=1, device_id=peer)
    pl.semaphore_signal(barrier, inc=1, device_id=other)

    flat[...] = x_ref[...].reshape(DEPTH, NC).astype(jnp.float32)
    for c, bins in enumerate(CLASSES):
        tail = 8 * LANE + c // 4 * LANE + c % 4 * 16
        for part in range(2):
            for i, f in enumerate(bins):
                start = part * NW * NF + f
                place = c * LANE + part * 64 + i * NW
                if i < 3:
                    ordered[pl.ds(place, NW), :] = flat[pl.ds(start, NW, stride=NF), :]
                else:
                    ordered[pl.ds(place, 4), :] = flat[pl.ds(start, 4, stride=NF), :]
                    ordered[pl.ds(tail + part * 64, 16), :] = flat[pl.ds(start + 4 * NF, 16, stride=NF), :]
    for t in range(10):
        own[:, t * LANE:(t + 1) * LANE] = ordered[t * LANE:(t + 1) * LANE, :].T.astype(jnp.bfloat16)

    keep = pltpu.make_async_copy(own, all_ref.at[row], local_sem)
    keep.start()

    def first_copy(src, index, slot, piece, device):
        return pltpu.make_async_remote_copy(
            src_ref=src, dst_ref=first_ref.at[slot, pl.ds(piece * size, size)], send_sem=first_send.at[index],
            recv_sem=first_recv.at[index], device_id=device,
        )

    def part(index, sem):
        place = first_ref.at[index // PIECES, pl.ds(index % PIECES * size, size)]
        return pltpu.make_async_copy(place, place, sem)

    def serve(piece, offset):
        origin = source(offset)
        rows = pl.ds(piece * size, size)
        src = own.at[rows] if offset == 0 else all_ref.at[origin, rows]
        slot = origin % 4
        index = slot * PIECES + piece
        wanted = origin // 4 == line

        @pl.when(jnp.logical_and(wanted, passes))
        def _():
            first_copy(src, index, slot, piece, other).start()

        @pl.when(jnp.logical_and(wanted, keeps))
        def _():
            first_copy(src, index, slot, piece, peer).start()
            pltpu.make_async_copy(src, first_ref.at[slot, rows], first_recv.at[index]).start()

    def move(plan):
        pl.semaphore_wait(barrier, len(steps_of(plan)) + 2)
        sent = []
        seen = set()
        for n, (step, piece, offset) in enumerate(plan):
            rows = pl.ds(piece * size, size)
            place = all_ref.at[source(offset), rows]
            fresh = (piece, offset) not in seen
            seen.add((piece, offset))
            if fresh and offset:
                pltpu.make_async_copy(place, place, recv_sem.at[piece * NR + offset]).wait()
            if step >= 0:
                copy = pltpu.make_async_remote_copy(
                    src_ref=own.at[rows] if offset == 0 else place,
                    dst_ref=place,
                    send_sem=send_sem.at[len(sent)],
                    recv_sem=recv_sem.at[piece * NR + shifted(offset, STEPS[step])],
                    device_id={"row": there(STEPS[step]), "col": col},
                )
                copy.start()
                sent.append(copy)
            if fresh:
                serve(piece, offset)
        assert len(seen) == PIECES * NR and len(sent) == PIECES * (NR - 1)
        return sent

    for which, plan in enumerate(PLANS):

        @pl.when(core == which)
        def _():
            sent = move(plan)
            for index in range(4 * PIECES):
                part(index, first_recv.at[index]).wait()

                @pl.when(passes)
                def _():
                    pltpu.make_async_remote_copy(
                        src_ref=first_ref.at[index // PIECES, pl.ds(index % PIECES * size, size)],
                        dst_ref=first_ref.at[index // PIECES, pl.ds(index % PIECES * size, size)],
                        send_sem=first_send.at[4 * PIECES + index], recv_sem=first_recv.at[index], device_id=peer,
                    ).start()

            for copy in sent:
                copy.wait_send()

    keep.wait()

    @pl.when(serves)
    def _():
        for index in range(4 * PIECES):
            part(index, first_send.at[index]).wait()

    @pl.when(passes)
    def _():
        for index in range(4 * PIECES):
            part(index, first_send.at[4 * PIECES + index]).wait()


def butterflies(zero, eight, real, imag):
    c1, c2, c3 = (math.cos(math.pi * k / 8) for k in (1, 2, 3))
    e = [zero] + real + [eight]
    u0, u1, u2, u3, u4 = e[0] + e[8], e[1] + e[7], e[2] + e[6], e[3] + e[5], e[4]
    d0, d1, d2, d3 = e[0] - e[8], e[1] - e[7], e[2] - e[6], e[3] - e[5]
    v0, v1 = u0 + u4, u1 + u3
    w0, w1 = u0 - u4, c2 * (u1 - u3)
    g = c2 * d2
    h0, h1 = d0 + g, d0 - g
    p, q = c1 * d1 + c3 * d3, c3 * d1 - c1 * d3
    v2 = v0 + u2
    even = [v2 + v1, h0 + p, w0 + w1, h1 + q, v0 - u2, h1 - q, w0 - w1, h0 - p, v2 - v1]
    f = [None] + imag
    s1, s2, s3 = f[1] + f[7], f[2] + f[6], f[3] + f[5]
    t1, t2, t3 = f[1] - f[7], f[2] - f[6], f[3] - f[5]
    g = c2 * s2
    a, b = c3 * s1 + c1 * s3, c1 * s1 - c3 * s3
    g0, g1 = g + f[4], g - f[4]
    k = c2 * (t1 + t3)
    odd = [None, a + g0, k + t2, b + g1, t1 - t3, b - g1, k - t2, a - g0]
    out = [even[0]] + [even[m] - odd[m] for m in range(1, 8)] + [even[8]]
    return out + [even[m] + odd[m] for m in range(7, 0, -1)]


TILE = 256
BAND = 64
WIDE = 256


def product_kernel(first_ref, all_ref, out_ref, left, prod_0, prod_1, outs, sems):
    prods = (prod_0, prod_1)
    lane = lax.broadcasted_iota(jnp.int32, (LANE, LANE), 1)
    place = lane % 64
    turn = jnp.where(lane < 64, 1.0, -1.0)

    def choose(values, edges):
        out = jnp.full((LANE, LANE), values[-1], jnp.float32)
        for value, edge in zip(values[-2::-1], edges[::-1]):
            out = jnp.where(place < edge, value, out)
        return out

    def phases(t):
        if t < 8:
            bins, edges, signs = CLASSES[t], (20, 40, 60), (1.0, 1.0, -1.0, -1.0)
        else:
            bins, edges, signs = tuple(CLASSES[4 * (t - 8) + i][3] for i in range(4)), (16, 32, 48), (-1.0,) * 4
        angle = [2.0 * math.pi * f / NF for f in bins]
        cosine = choose([SCALE * math.cos(v) for v in angle], edges)
        sine = choose([SCALE * math.sin(v) for v in angle], edges) * turn
        return cosine, sine, choose(signs, edges) * -turn

    def variants(t):
        value = first_ref[:, t * LANE:(t + 1) * LANE].astype(jnp.float32)
        cosine, sine, sign = phases(t)
        turned = pltpu.roll(value, 64, 1)
        one = value * cosine + turned * sine
        return [value * SCALE, one], [turned * (sign * SCALE), pltpu.roll(one, 64, 1) * sign]

    def prepare(c, tail):
        plain, turned = variants(c)
        tail_plain, tail_turned = tail
        here = place // 16 == c % 4
        for lag in range(2):
            if c == 0:
                real = [jnp.where(place < 40, plain[lag], 0.0), jnp.zeros_like(plain[lag])]
                imag = [jnp.where(place < 40, 0.0, plain[lag]), jnp.where(here, tail_plain[lag], 0.0)]
            else:
                real = [plain[lag], jnp.where(here, tail_plain[lag], 0.0)]
                imag = [turned[lag], jnp.where(here, tail_turned[lag], 0.0)]
            for kind, pair in enumerate((real, imag)):
                rows = slice((kind * 2 + lag) * LANE, (kind * 2 + lag + 1) * LANE)
                left[c, rows, :LANE] = pair[0].astype(jnp.bfloat16)
                left[c, rows, LANE:] = pair[1].astype(jnp.bfloat16)

    def multiply(prod, tile, c):
        rows = pl.ds(tile * TILE, TILE)
        if isinstance(c, int):
            main, tail = pl.ds(c * LANE, LANE), pl.ds((8 + c // 4) * LANE, LANE)
        else:
            main = pl.ds(pl.multiple_of(c * LANE, LANE), LANE)
            tail = pl.ds(pl.multiple_of((8 + c // 4) * LANE, LANE), LANE)
        right = jnp.concatenate([all_ref[rows, main], all_ref[rows, tail]], axis=1)
        prod[c] = lax.dot_general(left[c], right, (((1,), (1,)), ((), ())), preferred_element_type=jnp.float32)

    def combine(prod, slot, band):
        for block in range(BAND // 8):
            start = pl.multiple_of(band * BAND + block * 8, 8)
            for lag in range(2):
                for half in range(TILE // WIDE):
                    span = slice(half * WIDE, (half + 1) * WIDE)
                    real = [prod[c, pl.ds(lag * LANE + start, 8), span] for c in range(8)]
                    imag = [prod[c, pl.ds((2 + lag) * LANE + start, 8), span] for c in range(8)]
                    lags = butterflies(real[0], imag[0], real[1:], imag[1:])
                    for m in range(16):
                        outs[slot, lag + 2 * m, pl.ds(start, 8), span] = lags[m]

    def writes(tile, band):
        rows = pl.ds(band * BAND, BAND)
        return pltpu.make_async_copy(
            outs.at[tile % 2, :, rows], out_ref.at[:, rows, pl.ds(tile * TILE, TILE)], sems.at[tile % 2, band]
        )

    bands = LANE // BAND
    tiles = out_ref.shape[2] // TILE
    tails = [variants(8), variants(9)]
    for c in range(8):
        prepare(c, tails[c // 4])
        multiply(prods[0], 0, c)
    for tile in range(tiles):

        @pl.loop(0, bands)
        def _(band):
            if tile >= 2:
                writes(tile - 2, band).wait()
            if tile + 1 < tiles:
                for i in range(8 // bands):
                    multiply(prods[(tile + 1) % 2], tile + 1, band * (8 // bands) + i)
            combine(prods[tile % 2], tile % 2, band)
            writes(tile, band).start()

    for tile in range(max(tiles - 2, 0), tiles):
        for band in range(bands):
            writes(tile, band).wait()


def product_call(first, gathered):
    return pl.pallas_call(
        product_kernel,
        out_shape=jax.ShapeDtypeStruct((NF, 4 * NC, NR * NC), jnp.float32),
        in_specs=[pl.BlockSpec(memory_space=pltpu.VMEM)] * 2,
        out_specs=pl.BlockSpec(memory_space=pl.ANY),
        scratch_shapes=[
            pltpu.VMEM((8, 4 * LANE, 2 * LANE), jnp.bfloat16),
            pltpu.VMEM((8, 4 * LANE, TILE), jnp.float32),
            pltpu.VMEM((8, 4 * LANE, TILE), jnp.float32),
            pltpu.VMEM((2, NF, LANE, TILE), jnp.float32),
            pltpu.SemaphoreType.DMA((2, LANE // BAND)),
        ],
        compiler_params=pltpu.CompilerParams(vmem_limit_bytes=40 * 1024 * 1024),
        name="product",
    )(first, gathered)


def on_device(spectra):
    gathered, first = pl.pallas_call(
        gather_kernel,
        out_shape=(
            jax.ShapeDtypeStruct((NR, NC, DEPTH), jnp.bfloat16),
            jax.ShapeDtypeStruct((4, NC, DEPTH), jnp.bfloat16),
        ),
        in_specs=[pl.BlockSpec(memory_space=pltpu.VMEM)],
        out_specs=(pl.BlockSpec(memory_space=pl.ANY), pl.BlockSpec(memory_space=pl.ANY)),
        scratch_shapes=[
            pltpu.VMEM((DEPTH, NC), jnp.float32),
            pltpu.VMEM((DEPTH, NC), jnp.float32),
            pltpu.VMEM((NC, DEPTH), jnp.bfloat16),
            pltpu.SemaphoreType.DMA((PIECES * (NR - 1),)),
            pltpu.SemaphoreType.DMA((PIECES * NR,)),
            pltpu.SemaphoreType.DMA((8 * PIECES,)),
            pltpu.SemaphoreType.DMA((4 * PIECES,)),
            pltpu.SemaphoreType.DMA,
        ],
        compiler_params=pltpu.CompilerParams(
            collective_id=0, has_side_effects=True, vmem_limit_bytes=16 * 1024 * 1024
        ),
        name="gather",
    )(spectra)
    return product_call(first.reshape(4 * NC, DEPTH), gathered.reshape(NR * NC, DEPTH))


def solution(mesh):
    return jax.shard_map(
        on_device,
        mesh=mesh,
        in_specs=(P(None, None, None, ("col", "row")),),
        out_specs=P(None, "row", "col"),
        check_vma=False,
    )
```

```python
import functools
import math

import jax
import jax.numpy as jnp
from jax import lax
from jax.experimental import pallas as pl
from jax.experimental.pallas import tpu as pltpu
from jax.sharding import PartitionSpec as P

NW, NF, NC, NR = 20, 32, 32, 32
DEPTH = 2 * NW * NF
LANE = 128
SCALE = 1.0 / math.sqrt(float(DEPTH))

PLAN_0 = (
    (1, 1, 0), (3, 1, 0), (4, 1, 0), (0, 0, 0), (2, 1, 0), (2, 0, 0), (0, 1, 0), (6, 0, 0),
    (1, 0, 0), (3, 0, 0), (4, 0, 0), (7, 1, 1), (1, 1, 1), (0, 1, 4), (3, 1, 4), (1, 1, 12),
    (2, 1, 12), (0, 1, 3), (1, 0, 16), (4, 0, 1), (3, 0, 5), (2, 0, 4), (0, 0, 5), (4, 0, 12),
    (1, 0, 5), (3, 0, 16), (2, 0, 12), (0, 1, 1), (4, 0, 16), (2, 0, 3), (1, 1, 4), (2, 0, 16),
    (2, 1, 4), (0, 1, 12), (4, 1, 2), (3, 1, 2), (1, 1, 9), (0, 1, 9), (-1, 1, 8), (4, 1, 15),
    (3, 1, 20), (1, 0, 13), (2, 1, 19), (1, 0, 9), (3, 0, 7), (0, 0, 8), (-1, 0, 6), (-1, 1, 13),
    (1, 0, 21), (0, 0, 15), (2, 1, 20), (-1, 1, 5), (4, 1, 19), (-1, 0, 2), (6, 1, 17), (0, 1, 14),
    (0, 1, 10), (4, 1, 17), (2, 1, 24), (-1, 1, 11), (-1, 1, 7), (1, 1, 20), (0, 0, 14), (-1, 0, 11),
    (-1, 1, 6), (3, 0, 21), (4, 0, 17), (-1, 0, 10), (2, 0, 20), (1, 0, 17), (3, 0, 22), (2, 0, 24),
    (-1, 1, 22), (-1, 1, 25), (-1, 1, 23), (-1, 1, 29), (-1, 0, 31), (-1, 0, 19), (-1, 1, 27), (-1, 1, 28),
    (-1, 0, 28), (-1, 1, 26), (-1, 1, 30), (-1, 1, 31), (-1, 0, 25), (-1, 1, 16), (-1, 1, 21), (-1, 1, 18),
    (-1, 0, 23), (-1, 0, 29), (-1, 0, 18), (-1, 0, 30), (-1, 0, 26), (-1, 0, 27),
)
PLAN_1 = (
    (4, 1, 0), (3, 1, 0), (0, 0, 0), (5, 1, 0), (5, 0, 0), (1, 0, 0), (0, 1, 0), (3, 0, 0),
    (4, 0, 0), (3, 1, 4), (2, 1, 4), (0, 1, 12), (8, 1, 12), (2, 1, 12), (3, 0, 16), (3, 0, 4),
    (0, 1, 4), (1, 0, 12), (4, 0, 16), (2, 0, 4), (0, 1, 2), (4, 1, 2), (1, 1, 16), (2, 1, 2),
    (1, 1, 12), (3, 0, 2), (0, 0, 2), (3, 0, 1), (4, 0, 2), (2, 1, 7), (0, 1, 7), (-1, 1, 8),
    (3, 1, 7), (8, 1, 28), (3, 0, 20), (0, 1, 15), (1, 1, 9), (2, 0, 8), (4, 0, 13), (2, 1, 16),
    (2, 1, 0), (2, 0, 20), (1, 1, 28), (0, 0, 13), (1, 0, 20), (3, 0, 6), (4, 1, 9), (1, 1, 20),
    (0, 1, 14), (4, 0, 7), (3, 0, 18), (4, 1, 28), (1, 0, 18), (-1, 1, 11), (4, 0, 18), (0, 1, 6),
    (3, 0, 11), (-1, 1, 10), (2, 0, 18), (1, 0, 24), (-1, 0, 5), (-1, 0, 9), (2, 0, 24), (3, 1, 23),
    (0, 0, 10), (-1, 1, 5), (-1, 1, 1), (-1, 1, 13), (1, 1, 25), (2, 0, 28), (-1, 1, 3), (-1, 1, 18),
    (-1, 0, 14), (-1, 0, 3), (-1, 1, 31), (-1, 1, 30), (-1, 0, 22), (-1, 0, 15), (-1, 0, 21), (-1, 1, 29),
    (-1, 1, 24), (-1, 0, 23), (-1, 0, 19), (-1, 0, 29), (-1, 1, 21), (-1, 0, 17), (-1, 1, 22), (-1, 0, 25),
    (-1, 1, 19), (-1, 0, 30), (-1, 0, 27), (-1, 1, 27), (-1, 1, 17), (-1, 0, 26), (-1, 1, 26), (-1, 0, 31),
)
PLANS = (PLAN_0, PLAN_1)
PIECES = 2
STEPS = (
    (1, 0, 0), (0, 0, 1), (0, 0, 3), (0, 1, 0), (0, 3, 0), (0, 0, 2), (0, 1, 1), (0, 2, 0),
    (0, 3, 1),
)
PASS_BEFORE = 8


def steps_of(plan):
    return sorted({STEPS[entry[0]] for entry in plan if entry[0] >= 0})


def split_offset(offset):
    return offset // 16, offset // 4 % 4, offset % 4


def shifted(offset, step):
    x, z, y = split_offset(offset)
    return (x + step[0]) % 2 * 16 + (z + step[1]) % 4 * 4 + (y + step[2]) % 4


CLASSES = ((0, 16, 8, 24),) + tuple((r, r + 16, 16 - r, 32 - r) for r in range(1, 8))


def gather_kernel(x_ref, all_ref, first_ref, raw, flat, ordered, own, send_sem, recv_sem, first_send, first_recv, local_sem):
    row = lax.axis_index("row")
    col = lax.axis_index("col")
    x, z, y = row // 16, row // 4 % 4, row % 4
    far, core = col // 2, col % 2
    peer = {"row": row, "col": far * 2 + 1 - core}
    target_row = far * 16 + z * 4 + y
    target = {"row": target_row, "col": (1 - far) * 2 + core}
    second = {"row": target_row, "col": far * 2 + core}
    server = {"row": z % 2 * 16 + z * 4 + y, "col": x * 2 + core}
    speaks = core == z // 2
    serves = jnp.logical_and(speaks, x == z % 2)
    keeps = jnp.logical_and(serves, far == x)
    both = jnp.logical_and(serves, far != x)
    passes = jnp.logical_and(speaks, jnp.logical_not(keeps))
    size = NC // PIECES

    back_x = [(x + 2 - i) % 2 for i in range(2)]
    back_z = [(z + 4 - i) % 4 for i in range(4)]
    back_y = [(y + 4 - i) % 4 for i in range(4)]
    part_x, part_z = [v * 16 for v in back_x], [v * 4 for v in back_z]

    def there(step):
        return part_x[-step[0] % 2] + part_z[-step[1] % 4] + back_y[-step[2] % 4]

    def source(offset):
        ox, oz, oy = split_offset(offset)
        return part_x[ox] + part_z[oz] + back_y[oy]

    lines = [back_z[j] == y for j in range(4)]
    serve_line = [jnp.logical_and(serves, v) for v in lines]
    keep_line = [jnp.logical_and(keeps, v) for v in lines]
    both_line = [jnp.logical_and(both, v) for v in lines]

    load = pltpu.make_async_copy(x_ref, raw, local_sem)
    load.start()

    barrier = pltpu.get_barrier_semaphore()
    for which, plan in enumerate(PLANS):

        @pl.when(core == which)
        def _():
            for step in steps_of(plan):
                behind = ((-step[0]) % 2, (-step[1]) % 4, (-step[2]) % 4)
                pl.semaphore_signal(barrier, inc=1, device_id={"row": there(behind), "col": col})

    pl.semaphore_signal(barrier, inc=1, device_id=peer)

    @pl.when(passes)
    def _():
        pl.semaphore_signal(barrier, inc=1, device_id=server)

    load.wait()
    flat[...] = raw[...].reshape(DEPTH, NC).astype(jnp.float32)
    for c, bins in enumerate(CLASSES):
        tail = 8 * LANE + c // 4 * LANE + c % 4 * 16
        for part in range(2):
            for i, f in enumerate(bins):
                start = part * NW * NF + f
                place = c * LANE + part * 64 + i * NW
                if i < 3:
                    ordered[pl.ds(place, NW), :] = flat[pl.ds(start, NW, stride=NF), :]
                else:
                    ordered[pl.ds(place, 4), :] = flat[pl.ds(start, 4, stride=NF), :]
                    ordered[pl.ds(tail + part * 64, 16), :] = flat[pl.ds(start + 4 * NF, 16, stride=NF), :]
    for t in range(10):
        own[:, t * LANE:(t + 1) * LANE] = ordered[t * LANE:(t + 1) * LANE, :].T.astype(jnp.bfloat16)

    keep = pltpu.make_async_copy(own, all_ref.at[row], local_sem)
    keep.start()

    def first_copy(src, index, slot, piece, which, device):
        return pltpu.make_async_remote_copy(
            src_ref=src, dst_ref=first_ref.at[slot, pl.ds(piece * size, size)],
            send_sem=first_send.at[which * 4 * PIECES + index],
            recv_sem=first_recv.at[index], device_id=device,
        )

    def part(index, sem):
        place = first_ref.at[index // PIECES, pl.ds(index % PIECES * size, size)]
        return pltpu.make_async_copy(place, place, sem)

    def serve(piece, offset):
        ox, oz, oy = split_offset(offset)
        rows = pl.ds(piece * size, size)
        src = own.at[rows] if offset == 0 else all_ref.at[source(offset), rows]
        slot = back_y[oy]
        index = slot * PIECES + piece

        @pl.when(serve_line[oz])
        def _():
            first_copy(src, index, slot, piece, 0, target).start()

        @pl.when(both_line[oz])
        def _():
            first_copy(src, index, slot, piece, 1, second).start()

        @pl.when(keep_line[oz])
        def _():
            first_copy(src, index, slot, piece, 1, peer).start()
            pltpu.make_async_copy(src, first_ref.at[slot, rows], first_recv.at[index]).start()

    def pass_on():
        @pl.when(passes)
        def _():
            for index in range(4 * PIECES):
                slot, piece = index // PIECES, index % PIECES
                part(index, first_recv.at[index]).wait()
                first_copy(first_ref.at[slot, pl.ds(piece * size, size)], index, slot, piece, 2, peer).start()

    def move(plan):
        pl.semaphore_wait(barrier, len(steps_of(plan)) + 1 + jnp.where(both, 2, jnp.where(keeps, 1, 0)))
        sent = []
        seen = set()
        for n, (step, piece, offset) in enumerate(plan):
            rows = pl.ds(piece * size, size)
            place = all_ref.at[source(offset), rows]
            fresh = (piece, offset) not in seen
            seen.add((piece, offset))
            if fresh and offset:
                pltpu.make_async_copy(place, place, recv_sem.at[piece * NR + offset]).wait()
            if step >= 0:
                copy = pltpu.make_async_remote_copy(
                    src_ref=own.at[rows] if offset == 0 else place,
                    dst_ref=place,
                    send_sem=send_sem.at[len(sent)],
                    recv_sem=recv_sem.at[piece * NR + shifted(offset, STEPS[step])],
                    device_id={"row": there(STEPS[step]), "col": col},
                )
                copy.start()
                sent.append(copy)
            if fresh and offset < NR // 2:
                serve(piece, offset)
            if n == len(plan) - PASS_BEFORE:
                pass_on()
        assert len(seen) == PIECES * NR and len(sent) == PIECES * (NR - 1)
        return sent

    for which, plan in enumerate(PLANS):

        @pl.when(core == which)
        def _():
            sent = move(plan)

            @pl.when(jnp.logical_not(passes))
            def _():
                for index in range(4 * PIECES):
                    part(index, first_recv.at[index]).wait()

            for copy in sent:
                copy.wait_send()

    keep.wait()

    for which, taken in enumerate((serves, serves, passes)):

        @pl.when(taken)
        def _():
            for index in range(4 * PIECES):
                part(index, first_send.at[which * 4 * PIECES + index]).wait()


def butterflies(zero, eight, real, imag):
    c1, c2, c3 = (math.cos(math.pi * k / 8) for k in (1, 2, 3))
    e = [zero] + real + [eight]
    u0, u1, u2, u3, u4 = e[0] + e[8], e[1] + e[7], e[2] + e[6], e[3] + e[5], e[4]
    d0, d1, d2, d3 = e[0] - e[8], e[1] - e[7], e[2] - e[6], e[3] - e[5]
    v0, v1 = u0 + u4, u1 + u3
    w0, w1 = u0 - u4, c2 * (u1 - u3)
    g = c2 * d2
    h0, h1 = d0 + g, d0 - g
    p, q = c1 * d1 + c3 * d3, c3 * d1 - c1 * d3
    v2 = v0 + u2
    even = [v2 + v1, h0 + p, w0 + w1, h1 + q, v0 - u2, h1 - q, w0 - w1, h0 - p, v2 - v1]
    f = [None] + imag
    s1, s2, s3 = f[1] + f[7], f[2] + f[6], f[3] + f[5]
    t1, t2, t3 = f[1] - f[7], f[2] - f[6], f[3] - f[5]
    g = c2 * s2
    a, b = c3 * s1 + c1 * s3, c1 * s1 - c3 * s3
    g0, g1 = g + f[4], g - f[4]
    k = c2 * (t1 + t3)
    odd = [None, a + g0, k + t2, b + g1, t1 - t3, b - g1, k - t2, a - g0]
    out = [even[0]] + [even[m] - odd[m] for m in range(1, 8)] + [even[8]]
    return out + [even[m] + odd[m] for m in range(7, 0, -1)]


TILE = 256
BAND = 64
WIDE = 256


def product_kernel(first_ref, all_ref, out_ref, left, prod_0, prod_1, outs, sems):
    prods = (prod_0, prod_1)
    lane = lax.broadcasted_iota(jnp.int32, (LANE, LANE), 1)
    place = lane % 64
    turn = jnp.where(lane < 64, 1.0, -1.0)

    def choose(values, edges):
        out = jnp.full((LANE, LANE), values[-1], jnp.float32)
        for value, edge in zip(values[-2::-1], edges[::-1]):
            out = jnp.where(place < edge, value, out)
        return out

    def phases(t):
        if t < 8:
            bins, edges, signs = CLASSES[t], (20, 40, 60), (1.0, 1.0, -1.0, -1.0)
        else:
            bins, edges, signs = tuple(CLASSES[4 * (t - 8) + i][3] for i in range(4)), (16, 32, 48), (-1.0,) * 4
        angle = [2.0 * math.pi * f / NF for f in bins]
        cosine = choose([SCALE * math.cos(v) for v in angle], edges)
        sine = choose([SCALE * math.sin(v) for v in angle], edges) * turn
        return cosine, sine, choose(signs, edges) * -turn

    def variants(t):
        value = first_ref[:, t * LANE:(t + 1) * LANE].astype(jnp.float32)
        cosine, sine, sign = phases(t)
        turned = pltpu.roll(value, 64, 1)
        one = value * cosine + turned * sine
        return [value * SCALE, one], [turned * (sign * SCALE), pltpu.roll(one, 64, 1) * sign]

    def prepare(c, tail):
        plain, turned = variants(c)
        tail_plain, tail_turned = tail
        here = place // 16 == c % 4
        for lag in range(2):
            if c == 0:
                real = [jnp.where(place < 40, plain[lag], 0.0), jnp.zeros_like(plain[lag])]
                imag = [jnp.where(place < 40, 0.0, plain[lag]), jnp.where(here, tail_plain[lag], 0.0)]
            else:
                real = [plain[lag], jnp.where(here, tail_plain[lag], 0.0)]
                imag = [turned[lag], jnp.where(here, tail_turned[lag], 0.0)]
            for kind, pair in enumerate((real, imag)):
                rows = slice((kind * 2 + lag) * LANE, (kind * 2 + lag + 1) * LANE)
                left[c, rows, :LANE] = pair[0].astype(jnp.bfloat16)
                left[c, rows, LANE:] = pair[1].astype(jnp.bfloat16)

    def multiply(prod, tile, c):
        rows = pl.ds(tile * TILE, TILE)
        if isinstance(c, int):
            main, tail = pl.ds(c * LANE, LANE), pl.ds((8 + c // 4) * LANE, LANE)
        else:
            main = pl.ds(pl.multiple_of(c * LANE, LANE), LANE)
            tail = pl.ds(pl.multiple_of((8 + c // 4) * LANE, LANE), LANE)
        right = jnp.concatenate([all_ref[rows, main], all_ref[rows, tail]], axis=1)
        prod[c] = lax.dot_general(left[c], right, (((1,), (1,)), ((), ())), preferred_element_type=jnp.float32)

    def combine(prod, slot, band, part):
        for block in range(part * BAND // 32, (part + 1) * BAND // 32):
            start = pl.multiple_of(band * BAND + block * 8, 8)
            for lag in range(2):
                for half in range(TILE // WIDE):
                    span = slice(half * WIDE, (half + 1) * WIDE)
                    real = [prod[c, pl.ds(lag * LANE + start, 8), span] for c in range(8)]
                    imag = [prod[c, pl.ds((2 + lag) * LANE + start, 8), span] for c in range(8)]
                    lags = butterflies(real[0], imag[0], real[1:], imag[1:])
                    for m in range(16):
                        outs[slot, lag + 2 * m, pl.ds(start, 8), span] = lags[m]

    def writes(tile, band):
        rows = pl.ds(band * BAND, BAND)
        return pltpu.make_async_copy(
            outs.at[tile % 2, :, rows], out_ref.at[:, rows, pl.ds(tile * TILE, TILE)], sems.at[tile % 2, band]
        )

    bands = LANE // BAND
    tiles = out_ref.shape[2] // TILE
    tails = [variants(8), variants(9)]
    for c in range(8):
        prepare(c, tails[c // 4])
        multiply(prods[0], 0, c)
    for tile in range(tiles):

        for band in range(bands):
            if tile >= 2:
                writes(tile - 2, band).wait()
            for i in range(8 // bands):
                if tile + 1 < tiles:
                    multiply(prods[(tile + 1) % 2], tile + 1, band * (8 // bands) + i)
                combine(prods[tile % 2], tile % 2, band, i)
            writes(tile, band).start()

    for tile in range(max(tiles - 2, 0), tiles):
        for band in range(bands):
            writes(tile, band).wait()


def product_call(first, gathered):
    return pl.pallas_call(
        product_kernel,
        out_shape=jax.ShapeDtypeStruct((NF, 4 * NC, NR * NC), jnp.float32),
        in_specs=[pl.BlockSpec(memory_space=pltpu.VMEM)] * 2,
        out_specs=pl.BlockSpec(memory_space=pl.ANY),
        scratch_shapes=[
            pltpu.VMEM((8, 4 * LANE, 2 * LANE), jnp.bfloat16),
            pltpu.VMEM((8, 4 * LANE, TILE), jnp.float32),
            pltpu.VMEM((8, 4 * LANE, TILE), jnp.float32),
            pltpu.VMEM((2, NF, LANE, TILE), jnp.float32),
            pltpu.SemaphoreType.DMA((2, LANE // BAND)),
        ],
        compiler_params=pltpu.CompilerParams(vmem_limit_bytes=40 * 1024 * 1024),
        name="product",
    )(first, gathered)


def on_device(spectra):
    gathered, first = pl.pallas_call(
        gather_kernel,
        out_shape=(
            jax.ShapeDtypeStruct((NR, NC, DEPTH), jnp.bfloat16),
            jax.ShapeDtypeStruct((4, NC, DEPTH), jnp.bfloat16),
        ),
        in_specs=[pl.BlockSpec(memory_space=pltpu.HBM)],
        out_specs=(pl.BlockSpec(memory_space=pl.ANY), pl.BlockSpec(memory_space=pl.ANY)),
        scratch_shapes=[
            pltpu.VMEM((2, NW, NF, NC), jnp.bfloat16),
            pltpu.VMEM((DEPTH, NC), jnp.float32),
            pltpu.VMEM((DEPTH, NC), jnp.float32),
            pltpu.VMEM((NC, DEPTH), jnp.bfloat16),
            pltpu.SemaphoreType.DMA((PIECES * (NR - 1),)),
            pltpu.SemaphoreType.DMA((PIECES * NR,)),
            pltpu.SemaphoreType.DMA((12 * PIECES,)),
            pltpu.SemaphoreType.DMA((4 * PIECES,)),
            pltpu.SemaphoreType.DMA,
        ],
        compiler_params=pltpu.CompilerParams(
            collective_id=0, has_side_effects=True, vmem_limit_bytes=16 * 1024 * 1024
        ),
        name="gather",
    )(pltpu.with_memory_space_constraint(spectra, pltpu.HBM))
    return product_call(first.reshape(4 * NC, DEPTH), gathered.reshape(NR * NC, DEPTH))


def solution(mesh):
    return jax.shard_map(
        on_device,
        mesh=mesh,
        in_specs=(P(None, None, None, ("col", "row")),),
        out_specs=P(None, "row", "col"),
        check_vma=False,
    )
```

```python
import functools
import math

import jax
import jax.numpy as jnp
from jax import lax
from jax.experimental import pallas as pl
from jax.experimental.pallas import tpu as pltpu
from jax.sharding import PartitionSpec as P

NW, NF, NC, NR = 20, 32, 32, 32
DEPTH = 2 * NW * NF
LANE = 128
SCALE = 1.0 / math.sqrt(float(DEPTH))

PLAN_0 = (
    (1, 1, 0), (3, 1, 0), (4, 1, 0), (0, 0, 0), (2, 1, 0), (2, 0, 0), (0, 1, 0), (6, 0, 0),
    (1, 0, 0), (3, 0, 0), (4, 0, 0), (7, 1, 1), (1, 1, 1), (0, 1, 4), (3, 1, 4), (1, 1, 12),
    (2, 1, 12), (0, 1, 3), (1, 0, 16), (4, 0, 1), (3, 0, 5), (2, 0, 4), (0, 0, 5), (4, 0, 12),
    (1, 0, 5), (3, 0, 16), (2, 0, 12), (0, 1, 1), (4, 0, 16), (2, 0, 3), (1, 1, 4), (2, 0, 16),
    (2, 1, 4), (0, 1, 12), (4, 1, 2), (3, 1, 2), (1, 1, 9), (0, 1, 9), (-1, 1, 8), (4, 1, 15),
    (3, 1, 20), (1, 0, 13), (2, 1, 19), (1, 0, 9), (3, 0, 7), (0, 0, 8), (-1, 0, 6), (-1, 1, 13),
    (1, 0, 21), (0, 0, 15), (2, 1, 20), (-1, 1, 5), (4, 1, 19), (-1, 0, 2), (6, 1, 17), (0, 1, 14),
    (0, 1, 10), (4, 1, 17), (2, 1, 24), (-1, 1, 11), (-1, 1, 7), (1, 1, 20), (0, 0, 14), (-1, 0, 11),
    (-1, 1, 6), (3, 0, 21), (4, 0, 17), (-1, 0, 10), (2, 0, 20), (1, 0, 17), (3, 0, 22), (2, 0, 24),
    (-1, 1, 22), (-1, 1, 25), (-1, 1, 23), (-1, 1, 29), (-1, 0, 31), (-1, 0, 19), (-1, 1, 27), (-1, 1, 28),
    (-1, 0, 28), (-1, 1, 26), (-1, 1, 30), (-1, 1, 31), (-1, 0, 25), (-1, 1, 16), (-1, 1, 21), (-1, 1, 18),
    (-1, 0, 23), (-1, 0, 29), (-1, 0, 18), (-1, 0, 30), (-1, 0, 26), (-1, 0, 27),
)
PLAN_1 = (
    (4, 1, 0), (3, 1, 0), (0, 0, 0), (5, 1, 0), (5, 0, 0), (1, 0, 0), (0, 1, 0), (3, 0, 0),
    (4, 0, 0), (3, 1, 4), (2, 1, 4), (0, 1, 12), (8, 1, 12), (2, 1, 12), (3, 0, 16), (3, 0, 4),
    (0, 1, 4), (1, 0, 12), (4, 0, 16), (2, 0, 4), (0, 1, 2), (4, 1, 2), (1, 1, 16), (2, 1, 2),
    (1, 1, 12), (3, 0, 2), (0, 0, 2), (3, 0, 1), (4, 0, 2), (2, 1, 7), (0, 1, 7), (-1, 1, 8),
    (3, 1, 7), (8, 1, 28), (3, 0, 20), (0, 1, 15), (1, 1, 9), (2, 0, 8), (4, 0, 13), (2, 1, 16),
    (2, 1, 0), (2, 0, 20), (1, 1, 28), (0, 0, 13), (1, 0, 20), (3, 0, 6), (4, 1, 9), (1, 1, 20),
    (0, 1, 14), (4, 0, 7), (3, 0, 18), (4, 1, 28), (1, 0, 18), (-1, 1, 11), (4, 0, 18), (0, 1, 6),
    (3, 0, 11), (-1, 1, 10), (2, 0, 18), (1, 0, 24), (-1, 0, 5), (-1, 0, 9), (2, 0, 24), (3, 1, 23),
    (0, 0, 10), (-1, 1, 5), (-1, 1, 1), (-1, 1, 13), (1, 1, 25), (2, 0, 28), (-1, 1, 3), (-1, 1, 18),
    (-1, 0, 14), (-1, 0, 3), (-1, 1, 31), (-1, 1, 30), (-1, 0, 22), (-1, 0, 15), (-1, 0, 21), (-1, 1, 29),
    (-1, 1, 24), (-1, 0, 23), (-1, 0, 19), (-1, 0, 29), (-1, 1, 21), (-1, 0, 17), (-1, 1, 22), (-1, 0, 25),
    (-1, 1, 19), (-1, 0, 30), (-1, 0, 27), (-1, 1, 27), (-1, 1, 17), (-1, 0, 26), (-1, 1, 26), (-1, 0, 31),
)
PLANS = (PLAN_0, PLAN_1)
PIECES = 2
STEPS = (
    (1, 0, 0), (0, 0, 1), (0, 0, 3), (0, 1, 0), (0, 3, 0), (0, 0, 2), (0, 1, 1), (0, 2, 0),
    (0, 3, 1),
)
PASS_BEFORE = 14


def ends_of(plan):
    onward = {entry[1:] for entry in plan if entry[0] >= 0}
    every = {(piece, offset) for piece in range(PIECES) for offset in range(NR // 2, NR)}
    return every - onward


def steps_of(plan):
    return sorted({STEPS[entry[0]] for entry in plan if entry[0] >= 0})


def split_offset(offset):
    return offset // 16, offset // 4 % 4, offset % 4


def shifted(offset, step):
    x, z, y = split_offset(offset)
    return (x + step[0]) % 2 * 16 + (z + step[1]) % 4 * 4 + (y + step[2]) % 4


CLASSES = ((0, 16, 8, 24),) + tuple((r, r + 16, 16 - r, 32 - r) for r in range(1, 8))


def gather_kernel(x_ref, all_ref, first_ref, raw, flat, ordered, own, send_sem, recv_sem, first_send, first_recv, local_sem):
    row = lax.axis_index("row")
    col = lax.axis_index("col")
    x, z, y = row // 16, row // 4 % 4, row % 4
    far, core = col // 2, col % 2
    peer = {"row": row, "col": far * 2 + 1 - core}
    target_row = far * 16 + z * 4 + y
    target = {"row": target_row, "col": (1 - far) * 2 + core}
    second = {"row": target_row, "col": far * 2 + core}
    server = {"row": z % 2 * 16 + z * 4 + y, "col": x * 2 + core}
    speaks = core == z // 2
    serves = jnp.logical_and(speaks, x == z % 2)
    keeps = jnp.logical_and(serves, far == x)
    both = jnp.logical_and(serves, far != x)
    passes = jnp.logical_and(speaks, jnp.logical_not(keeps))
    size = NC // PIECES

    back_x = [(x + 2 - i) % 2 for i in range(2)]
    back_z = [(z + 4 - i) % 4 for i in range(4)]
    back_y = [(y + 4 - i) % 4 for i in range(4)]
    part_x, part_z = [v * 16 for v in back_x], [v * 4 for v in back_z]

    def there(step):
        return part_x[-step[0] % 2] + part_z[-step[1] % 4] + back_y[-step[2] % 4]

    def source(offset):
        ox, oz, oy = split_offset(offset)
        return part_x[ox] + part_z[oz] + back_y[oy]

    lines = [back_z[j] == y for j in range(4)]
    serve_line = [jnp.logical_and(serves, v) for v in lines]

    load = pltpu.make_async_copy(x_ref, raw, local_sem)
    load.start()

    barrier = pltpu.get_barrier_semaphore()
    for which, plan in enumerate(PLANS):

        @pl.when(core == which)
        def _():
            for step in steps_of(plan):
                behind = ((-step[0]) % 2, (-step[1]) % 4, (-step[2]) % 4)
                pl.semaphore_signal(barrier, inc=1, device_id={"row": there(behind), "col": col})

    pl.semaphore_signal(barrier, inc=1, device_id=peer)

    @pl.when(passes)
    def _():
        pl.semaphore_signal(barrier, inc=1, device_id=server)

    load.wait()
    flat[...] = raw[...].reshape(DEPTH, NC).astype(jnp.float32)
    for c, bins in enumerate(CLASSES):
        tail = 8 * LANE + c // 4 * LANE + c % 4 * 16
        for part in range(2):
            for i, f in enumerate(bins):
                start = part * NW * NF + f
                place = c * LANE + part * 64 + i * NW
                if i < 3:
                    ordered[pl.ds(place, NW), :] = flat[pl.ds(start, NW, stride=NF), :]
                else:
                    ordered[pl.ds(place, 4), :] = flat[pl.ds(start, 4, stride=NF), :]
                    ordered[pl.ds(tail + part * 64, 16), :] = flat[pl.ds(start + 4 * NF, 16, stride=NF), :]
    for t in range(10):
        own[:, t * LANE:(t + 1) * LANE] = ordered[t * LANE:(t + 1) * LANE, :].T.astype(jnp.bfloat16)

    keep = pltpu.make_async_copy(own, all_ref.at[row], local_sem)
    keep.start()

    def first_copy(src, dst, which, device):
        return pltpu.make_async_remote_copy(
            src_ref=src, dst_ref=dst, send_sem=first_send.at[which], recv_sem=first_recv, device_id=device
        )

    def all_firsts(sem):
        pltpu.make_async_copy(first_ref, first_ref, sem).wait()

    def serve(piece, offset):
        ox, oz, oy = split_offset(offset)
        rows = pl.ds(piece * size, size)
        src = own.at[rows] if offset == 0 else all_ref.at[source(offset), rows]
        dst = first_ref.at[back_y[oy], rows]

        @pl.when(serve_line[oz])
        def _():
            first_copy(src, dst, 0, target).start()

            @pl.when(both)
            def _():
                first_copy(src, dst, 1, second).start()

            @pl.when(keeps)
            def _():
                first_copy(src, dst, 1, peer).start()
                pltpu.make_async_copy(src, dst, first_recv).start()

    def pass_on():
        @pl.when(passes)
        def _():
            all_firsts(first_recv)
            first_copy(first_ref, first_ref, 2, peer).start()

    def move(plan):
        pl.semaphore_wait(barrier, len(steps_of(plan)) + 1 + jnp.where(both, 2, jnp.where(keeps, 1, 0)))
        late = ends_of(plan)
        seen = set()
        for n, (step, piece, offset) in enumerate(plan):
            if n == len(plan) - PASS_BEFORE:
                pass_on()
            if (piece, offset) in late:
                continue
            rows = pl.ds(piece * size, size)
            place = all_ref.at[source(offset), rows]
            fresh = (piece, offset) not in seen
            seen.add((piece, offset))
            if fresh and offset:
                pltpu.make_async_copy(place, place, recv_sem.at[piece * NR + offset]).wait()
            if step >= 0:
                to = (piece, shifted(offset, STEPS[step]))
                pltpu.make_async_remote_copy(
                    src_ref=own.at[rows] if offset == 0 else place,
                    dst_ref=place,
                    send_sem=send_sem,
                    recv_sem=recv_sem.at[piece * NR + (0 if to in late else to[1])],
                    device_id={"row": there(STEPS[step]), "col": col},
                ).start()
            if fresh and offset < NR // 2:
                serve(piece, offset)
        assert len(seen) + len(late) == PIECES * NR
        for piece in range(PIECES):
            count = sum(1 for entry in late if entry[0] == piece)
            place = all_ref.at[pl.ds(0, count), pl.ds(piece * size, size)]
            pltpu.make_async_copy(place, place, recv_sem.at[piece * NR]).wait()

    for which, plan in enumerate(PLANS):

        @pl.when(core == which)
        def _():
            move(plan)

    @pl.when(jnp.logical_not(passes))
    def _():
        all_firsts(first_recv)

    place = all_ref.at[pl.ds(0, NR - 1)]
    pltpu.make_async_copy(place, place, send_sem).wait()
    keep.wait()

    for which, taken in enumerate((serves, serves, passes)):

        @pl.when(taken)
        def _():
            all_firsts(first_send.at[which])


def butterflies(zero, eight, real, imag):
    c1, c2, c3 = (math.cos(math.pi * k / 8) for k in (1, 2, 3))
    e = [zero] + real + [eight]
    u0, u1, u2, u3, u4 = e[0] + e[8], e[1] + e[7], e[2] + e[6], e[3] + e[5], e[4]
    d0, d1, d2, d3 = e[0] - e[8], e[1] - e[7], e[2] - e[6], e[3] - e[5]
    v0, v1 = u0 + u4, u1 + u3
    w0, w1 = u0 - u4, c2 * (u1 - u3)
    g = c2 * d2
    h0, h1 = d0 + g, d0 - g
    p, q = c1 * d1 + c3 * d3, c3 * d1 - c1 * d3
    v2 = v0 + u2
    even = [v2 + v1, h0 + p, w0 + w1, h1 + q, v0 - u2, h1 - q, w0 - w1, h0 - p, v2 - v1]
    f = [None] + imag
    s1, s2, s3 = f[1] + f[7], f[2] + f[6], f[3] + f[5]
    t1, t2, t3 = f[1] - f[7], f[2] - f[6], f[3] - f[5]
    g = c2 * s2
    a, b = c3 * s1 + c1 * s3, c1 * s1 - c3 * s3
    g0, g1 = g + f[4], g - f[4]
    k = c2 * (t1 + t3)
    odd = [None, a + g0, k + t2, b + g1, t1 - t3, b - g1, k - t2, a - g0]
    out = [even[0]] + [even[m] - odd[m] for m in range(1, 8)] + [even[8]]
    return out + [even[m] + odd[m] for m in range(7, 0, -1)]


TILE = 256
BAND = 64
WIDE = 256


def product_kernel(first_ref, all_ref, out_ref, left, prod_0, prod_1, outs, sems):
    prods = (prod_0, prod_1)
    lane = lax.broadcasted_iota(jnp.int32, (LANE, LANE), 1)
    place = lane % 64
    turn = jnp.where(lane < 64, 1.0, -1.0)

    def choose(values, edges):
        out = jnp.full((LANE, LANE), values[-1], jnp.float32)
        for value, edge in zip(values[-2::-1], edges[::-1]):
            out = jnp.where(place < edge, value, out)
        return out

    def phases(t):
        if t < 8:
            bins, edges, signs = CLASSES[t], (20, 40, 60), (1.0, 1.0, -1.0, -1.0)
        else:
            bins, edges, signs = tuple(CLASSES[4 * (t - 8) + i][3] for i in range(4)), (16, 32, 48), (-1.0,) * 4
        angle = [2.0 * math.pi * f / NF for f in bins]
        cosine = choose([SCALE * math.cos(v) for v in angle], edges)
        sine = choose([SCALE * math.sin(v) for v in angle], edges) * turn
        return cosine, sine, choose(signs, edges) * -turn

    def variants(t):
        value = first_ref[:, t * LANE:(t + 1) * LANE].astype(jnp.float32)
        cosine, sine, sign = phases(t)
        turned = pltpu.roll(value, 64, 1)
        one = value * cosine + turned * sine
        return [value * SCALE, one], [turned * (sign * SCALE), pltpu.roll(one, 64, 1) * sign]

    def prepare(c, tail):
        plain, turned = variants(c)
        tail_plain, tail_turned = tail
        here = place // 16 == c % 4
        for lag in range(2):
            if c == 0:
                real = [jnp.where(place < 40, plain[lag], 0.0), jnp.zeros_like(plain[lag])]
                imag = [jnp.where(place < 40, 0.0, plain[lag]), jnp.where(here, tail_plain[lag], 0.0)]
            else:
                real = [plain[lag], jnp.where(here, tail_plain[lag], 0.0)]
                imag = [turned[lag], jnp.where(here, tail_turned[lag], 0.0)]
            for kind, pair in enumerate((real, imag)):
                rows = slice((kind * 2 + lag) * LANE, (kind * 2 + lag + 1) * LANE)
                left[c, rows, :LANE] = pair[0].astype(jnp.bfloat16)
                left[c, rows, LANE:] = pair[1].astype(jnp.bfloat16)

    def multiply(prod, tile, c):
        rows = pl.ds(tile * TILE, TILE)
        if isinstance(c, int):
            main, tail = pl.ds(c * LANE, LANE), pl.ds((8 + c // 4) * LANE, LANE)
        else:
            main = pl.ds(pl.multiple_of(c * LANE, LANE), LANE)
            tail = pl.ds(pl.multiple_of((8 + c // 4) * LANE, LANE), LANE)
        right = jnp.concatenate([all_ref[rows, main], all_ref[rows, tail]], axis=1)
        prod[c] = lax.dot_general(left[c], right, (((1,), (1,)), ((), ())), preferred_element_type=jnp.float32)

    def combine(prod, slot, band, part):
        for block in range(part * BAND // 32, (part + 1) * BAND // 32):
            start = pl.multiple_of(band * BAND + block * 8, 8)
            for lag in range(2):
                for half in range(TILE // WIDE):
                    span = slice(half * WIDE, (half + 1) * WIDE)
                    real = [prod[c, pl.ds(lag * LANE + start, 8), span] for c in range(8)]
                    imag = [prod[c, pl.ds((2 + lag) * LANE + start, 8), span] for c in range(8)]
                    lags = butterflies(real[0], imag[0], real[1:], imag[1:])
                    for m in range(16):
                        outs[slot, lag + 2 * m, pl.ds(start, 8), span] = lags[m]

    def writes(tile, band):
        rows = pl.ds(band * BAND, BAND)
        return pltpu.make_async_copy(
            outs.at[tile % 2, :, rows], out_ref.at[:, rows, pl.ds(tile * TILE, TILE)], sems.at[tile % 2, band]
        )

    bands = LANE // BAND
    tiles = out_ref.shape[2] // TILE
    tails = [variants(8), variants(9)]
    for c in range(8):
        prepare(c, tails[c // 4])
        multiply(prods[0], 0, c)
    for tile in range(tiles):

        for band in range(bands):
            if tile >= 2:
                writes(tile - 2, band).wait()
            for i in range(8 // bands):
                if tile + 1 < tiles:
                    multiply(prods[(tile + 1) % 2], tile + 1, band * (8 // bands) + i)
                combine(prods[tile % 2], tile % 2, band, i)
            writes(tile, band).start()

    for tile in range(max(tiles - 2, 0), tiles):
        for band in range(bands):
            writes(tile, band).wait()


def product_call(first, gathered):
    return pl.pallas_call(
        product_kernel,
        out_shape=jax.ShapeDtypeStruct((NF, 4 * NC, NR * NC), jnp.float32),
        in_specs=[pl.BlockSpec(memory_space=pltpu.VMEM)] * 2,
        out_specs=pl.BlockSpec(memory_space=pl.ANY),
        scratch_shapes=[
            pltpu.VMEM((8, 4 * LANE, 2 * LANE), jnp.bfloat16),
            pltpu.VMEM((8, 4 * LANE, TILE), jnp.float32),
            pltpu.VMEM((8, 4 * LANE, TILE), jnp.float32),
            pltpu.VMEM((2, NF, LANE, TILE), jnp.float32),
            pltpu.SemaphoreType.DMA((2, LANE // BAND)),
        ],
        compiler_params=pltpu.CompilerParams(vmem_limit_bytes=40 * 1024 * 1024),
        name="product",
    )(first, gathered)


def on_device(spectra):
    gathered, first = pl.pallas_call(
        gather_kernel,
        out_shape=(
            jax.ShapeDtypeStruct((NR, NC, DEPTH), jnp.bfloat16),
            jax.ShapeDtypeStruct((4, NC, DEPTH), jnp.bfloat16),
        ),
        in_specs=[pl.BlockSpec(memory_space=pltpu.HBM)],
        out_specs=(pl.BlockSpec(memory_space=pl.ANY), pl.BlockSpec(memory_space=pl.ANY)),
        scratch_shapes=[
            pltpu.VMEM((2, NW, NF, NC), jnp.bfloat16),
            pltpu.VMEM((DEPTH, NC), jnp.float32),
            pltpu.VMEM((DEPTH, NC), jnp.float32),
            pltpu.VMEM((NC, DEPTH), jnp.bfloat16),
            pltpu.SemaphoreType.DMA,
            pltpu.SemaphoreType.DMA((PIECES * NR,)),
            pltpu.SemaphoreType.DMA((3,)),
            pltpu.SemaphoreType.DMA,
            pltpu.SemaphoreType.DMA,
        ],
        compiler_params=pltpu.CompilerParams(
            collective_id=0, has_side_effects=True, vmem_limit_bytes=16 * 1024 * 1024
        ),
        name="gather",
    )(pltpu.with_memory_space_constraint(spectra, pltpu.HBM))
    return product_call(first.reshape(4 * NC, DEPTH), gathered.reshape(NR * NC, DEPTH))


def solution(mesh):
    return jax.shard_map(
        on_device,
        mesh=mesh,
        in_specs=(P(None, None, None, ("col", "row")),),
        out_specs=P(None, "row", "col"),
        check_vma=False,
    )
```

```python
import functools
import math

import jax
import jax.numpy as jnp
from jax import lax
from jax.experimental import pallas as pl
from jax.experimental.pallas import tpu as pltpu
from jax.sharding import PartitionSpec as P

NW, NF, NC, NR = 20, 32, 32, 32
DEPTH = 2 * NW * NF
LANE = 128
SCALE = 1.0 / math.sqrt(float(DEPTH))

PLAN_0 = (
    (5, 0, 0), (4, 1, 0), (1, 0, 0), (2, 0, 0), (0, 0, 0), (3, 0, 0), (2, 1, 0), (5, 1, 0),
    (0, 1, 0), (1, 1, 0), (4, 0, 0), (4, 1, 12), (0, 1, 12), (3, 0, 3), (5, 0, 5), (0, 0, 3),
    (2, 0, 12), (4, 0, 12), (1, 0, 12), (2, 1, 3), (4, 0, 16), (0, 0, 5), (2, 1, 16), (1, 1, 5),
    (3, 1, 5), (3, 0, 16), (1, 0, 5), (1, 0, 1), (2, 1, 12), (0, 1, 1), (4, 1, 1), (3, 1, 3),
    (-1, 0, 4), (3, 0, 5), (0, 1, 5), (4, 1, 8), (2, 1, 8), (2, 1, 28), (4, 0, 15), (-1, 0, 8),
    (1, 0, 13), (-1, 0, 7), (0, 0, 10), (4, 1, 2), (1, 0, 16), (3, 1, 6), (4, 1, 28), (1, 0, 28),
    (2, 0, 28), (0, 1, 9), (3, 1, 16), (4, 0, 28), (-1, 1, 13), (0, 0, 6), (1, 1, 17), (2, 0, 20),
    (-1, 1, 15), (3, 0, 21), (-1, 1, 4), (3, 1, 19), (-1, 0, 2), (-1, 1, 11), (-1, 1, 7), (4, 1, 17),
    (2, 0, 19), (1, 1, 21), (-1, 0, 9), (-1, 0, 11), (-1, 0, 14), (4, 1, 31), (2, 1, 31), (-1, 1, 14),
    (1, 0, 26), (3, 0, 26), (0, 1, 10), (-1, 1, 20), (-1, 0, 24), (-1, 0, 22), (-1, 1, 25), (-1, 0, 31),
    (-1, 0, 29), (-1, 0, 25), (-1, 1, 22), (-1, 1, 18), (-1, 1, 23), (-1, 1, 29), (-1, 0, 17), (-1, 0, 18),
    (-1, 1, 30), (-1, 1, 24), (-1, 1, 27), (-1, 0, 23), (-1, 0, 27), (-1, 0, 30), (-1, 1, 26),
)
PLAN_1 = (
    (5, 1, 0), (2, 1, 0), (3, 1, 0), (6, 1, 0), (4, 0, 0), (5, 0, 0), (1, 0, 0), (0, 0, 0),
    (1, 1, 0), (2, 0, 0), (0, 1, 0), (4, 1, 3), (3, 0, 0), (2, 1, 3), (0, 1, 3), (3, 1, 5),
    (1, 1, 5), (4, 0, 3), (2, 1, 28), (1, 0, 16), (3, 0, 5), (4, 0, 12), (0, 1, 5), (2, 0, 16),
    (1, 0, 1), (3, 1, 3), (1, 0, 5), (3, 1, 4), (4, 1, 15), (2, 1, 15), (-1, 0, 4), (3, 0, 3),
    (4, 1, 1), (1, 1, 28), (2, 0, 15), (0, 1, 9), (2, 1, 19), (3, 0, 16), (4, 0, 15), (3, 1, 6),
    (4, 0, 1), (0, 0, 8), (1, 0, 9), (4, 0, 16), (4, 0, 17), (2, 0, 19), (1, 1, 21), (-1, 1, 2),
    (-1, 1, 7), (0, 1, 11), (2, 1, 21), (1, 1, 16), (-1, 1, 14), (0, 0, 6), (2, 1, 31), (-1, 0, 2),
    (3, 1, 8), (-1, 1, 13), (3, 1, 19), (-1, 0, 14), (4, 0, 19), (3, 0, 19), (2, 1, 25), (-1, 0, 7),
    (0, 0, 11), (1, 0, 24), (0, 0, 10), (1, 0, 20), (-1, 0, 13), (4, 0, 18), (2, 1, 27), (-1, 1, 10),
    (-1, 1, 12), (-1, 1, 30), (-1, 1, 18), (-1, 1, 23), (-1, 1, 17), (-1, 0, 27), (-1, 0, 31), (-1, 1, 20),
    (-1, 1, 24), (-1, 1, 22), (-1, 0, 22), (-1, 0, 29), (-1, 1, 29), (-1, 0, 25), (-1, 0, 28), (-1, 0, 23),
    (-1, 0, 21), (-1, 0, 26), (-1, 0, 30), (-1, 1, 26),
)
PLANS = (PLAN_0, PLAN_1)
PIECES = 2
STEPS = (
    (1, 0, 0), (0, 0, 1), (0, 0, 3), (0, 1, 0), (0, 3, 0), (0, 1, 1), (1, 3, 0),
)
PASS_BEFORE = 14


def ends_of(plan):
    onward = {entry[1:] for entry in plan if entry[0] >= 0}
    every = {(piece, offset) for piece in range(PIECES) for offset in range(NR // 2, NR)}
    return every - onward


def steps_of(plan):
    return sorted({STEPS[entry[0]] for entry in plan if entry[0] >= 0})


def split_offset(offset):
    return offset // 16, offset // 4 % 4, offset % 4


def shifted(offset, step):
    x, z, y = split_offset(offset)
    return (x + step[0]) % 2 * 16 + (z + step[1]) % 4 * 4 + (y + step[2]) % 4


CLASSES = ((0, 16, 8, 24),) + tuple((r, r + 16, 16 - r, 32 - r) for r in range(1, 8))


def gather_kernel(x_ref, all_ref, first_ref, raw, flat, ordered, own, send_sem, recv_sem, first_send, first_recv, local_sem):
    row = lax.axis_index("row")
    col = lax.axis_index("col")
    x, z, y = row // 16, row // 4 % 4, row % 4
    far, core = col // 2, col % 2
    peer = {"row": row, "col": far * 2 + 1 - core}
    target_row = far * 16 + z * 4 + y
    target = {"row": target_row, "col": (1 - far) * 2 + core}
    second = {"row": target_row, "col": far * 2 + core}
    server = {"row": z % 2 * 16 + z * 4 + y, "col": x * 2 + core}
    speaks = core == z // 2
    serves = jnp.logical_and(speaks, x == z % 2)
    keeps = jnp.logical_and(serves, far == x)
    both = jnp.logical_and(serves, far != x)
    passes = jnp.logical_and(speaks, jnp.logical_not(keeps))
    size = NC // PIECES

    back_x = [(x + 2 - i) % 2 for i in range(2)]
    back_z = [(z + 4 - i) % 4 for i in range(4)]
    back_y = [(y + 4 - i) % 4 for i in range(4)]
    part_x, part_z = [v * 16 for v in back_x], [v * 4 for v in back_z]

    def there(step):
        return part_x[-step[0] % 2] + part_z[-step[1] % 4] + back_y[-step[2] % 4]

    def source(offset):
        ox, oz, oy = split_offset(offset)
        return part_x[ox] + part_z[oz] + back_y[oy]

    lines = [back_z[j] == y for j in range(4)]
    serve_line = [jnp.logical_and(serves, v) for v in lines]

    load = pltpu.make_async_copy(x_ref, raw, local_sem)
    load.start()

    barrier = pltpu.get_barrier_semaphore()
    for which, plan in enumerate(PLANS):

        @pl.when(core == which)
        def _():
            for step in steps_of(plan):
                behind = ((-step[0]) % 2, (-step[1]) % 4, (-step[2]) % 4)
                pl.semaphore_signal(barrier, inc=1, device_id={"row": there(behind), "col": col})

    pl.semaphore_signal(barrier, inc=1, device_id=peer)

    @pl.when(passes)
    def _():
        pl.semaphore_signal(barrier, inc=1, device_id=server)

    load.wait()
    flat[...] = raw[...].reshape(DEPTH, NC).astype(jnp.float32)
    for c, bins in enumerate(CLASSES):
        tail = 8 * LANE + c // 4 * LANE + c % 4 * 16
        for part in range(2):
            for i, f in enumerate(bins):
                start = part * NW * NF + f
                place = c * LANE + part * 64 + i * NW
                if i < 3:
                    ordered[pl.ds(place, NW), :] = flat[pl.ds(start, NW, stride=NF), :]
                else:
                    ordered[pl.ds(place, 4), :] = flat[pl.ds(start, 4, stride=NF), :]
                    ordered[pl.ds(tail + part * 64, 16), :] = flat[pl.ds(start + 4 * NF, 16, stride=NF), :]
    for t in range(10):
        own[:, t * LANE:(t + 1) * LANE] = ordered[t * LANE:(t + 1) * LANE, :].T.astype(jnp.bfloat16)

    keep = pltpu.make_async_copy(own, all_ref.at[row], local_sem)
    keep.start()

    def first_copy(src, dst, which, device):
        return pltpu.make_async_remote_copy(
            src_ref=src, dst_ref=dst, send_sem=first_send.at[which], recv_sem=first_recv, device_id=device
        )

    def all_firsts(sem):
        pltpu.make_async_copy(first_ref, first_ref, sem).wait()

    def serve(piece, offset):
        ox, oz, oy = split_offset(offset)
        rows = pl.ds(piece * size, size)
        src = own.at[rows] if offset == 0 else all_ref.at[source(offset), rows]
        dst = first_ref.at[back_y[oy], rows]

        @pl.when(serve_line[oz])
        def _():
            first_copy(src, dst, 0, target).start()

            @pl.when(both)
            def _():
                first_copy(src, dst, 1, second).start()

            @pl.when(keeps)
            def _():
                first_copy(src, dst, 1, peer).start()
                pltpu.make_async_copy(src, dst, first_recv).start()

    def pass_on():
        @pl.when(passes)
        def _():
            all_firsts(first_recv)
            first_copy(first_ref, first_ref, 2, peer).start()

    def move(plan):
        pl.semaphore_wait(barrier, len(steps_of(plan)) + 1 + jnp.where(both, 2, jnp.where(keeps, 1, 0)))
        late = ends_of(plan)
        seen = set()
        for n, (step, piece, offset) in enumerate(plan):
            if n == len(plan) - PASS_BEFORE:
                pass_on()
            if (piece, offset) in late:
                continue
            rows = pl.ds(piece * size, size)
            place = all_ref.at[source(offset), rows]
            fresh = (piece, offset) not in seen
            seen.add((piece, offset))
            if fresh and offset:
                pltpu.make_async_copy(place, place, recv_sem.at[piece * NR + offset]).wait()
            if step >= 0:
                to = (piece, shifted(offset, STEPS[step]))
                pltpu.make_async_remote_copy(
                    src_ref=own.at[rows] if offset == 0 else place,
                    dst_ref=place,
                    send_sem=send_sem,
                    recv_sem=recv_sem.at[piece * NR + (0 if to in late else to[1])],
                    device_id={"row": there(STEPS[step]), "col": col},
                ).start()
            if fresh and offset < NR // 2:
                serve(piece, offset)
        assert len(seen) + len(late) == PIECES * NR
        for piece in range(PIECES):
            count = sum(1 for entry in late if entry[0] == piece)
            place = all_ref.at[pl.ds(0, count), pl.ds(piece * size, size)]
            pltpu.make_async_copy(place, place, recv_sem.at[piece * NR]).wait()

    for which, plan in enumerate(PLANS):

        @pl.when(core == which)
        def _():
            move(plan)

    @pl.when(jnp.logical_not(passes))
    def _():
        all_firsts(first_recv)

    place = all_ref.at[pl.ds(0, NR - 1)]
    pltpu.make_async_copy(place, place, send_sem).wait()
    keep.wait()

    for which, taken in enumerate((serves, serves, passes)):

        @pl.when(taken)
        def _():
            all_firsts(first_send.at[which])


def butterflies(zero, eight, real, imag):
    c1, c2, c3 = (math.cos(math.pi * k / 8) for k in (1, 2, 3))
    e = [zero] + real + [eight]
    u0, u1, u2, u3, u4 = e[0] + e[8], e[1] + e[7], e[2] + e[6], e[3] + e[5], e[4]
    d0, d1, d2, d3 = e[0] - e[8], e[1] - e[7], e[2] - e[6], e[3] - e[5]
    v0, v1 = u0 + u4, u1 + u3
    w0, w1 = u0 - u4, c2 * (u1 - u3)
    g = c2 * d2
    h0, h1 = d0 + g, d0 - g
    p, q = c1 * d1 + c3 * d3, c3 * d1 - c1 * d3
    v2 = v0 + u2
    even = [v2 + v1, h0 + p, w0 + w1, h1 + q, v0 - u2, h1 - q, w0 - w1, h0 - p, v2 - v1]
    f = [None] + imag
    s1, s2, s3 = f[1] + f[7], f[2] + f[6], f[3] + f[5]
    t1, t2, t3 = f[1] - f[7], f[2] - f[6], f[3] - f[5]
    g = c2 * s2
    a, b = c3 * s1 + c1 * s3, c1 * s1 - c3 * s3
    g0, g1 = g + f[4], g - f[4]
    k = c2 * (t1 + t3)
    odd = [None, a + g0, k + t2, b + g1, t1 - t3, b - g1, k - t2, a - g0]
    out = [even[0]] + [even[m] - odd[m] for m in range(1, 8)] + [even[8]]
    return out + [even[m] + odd[m] for m in range(7, 0, -1)]


TILE = 256
BAND = 64
WIDE = 256


def product_kernel(first_ref, all_ref, out_ref, left, prod_0, prod_1, outs, sems):
    prods = (prod_0, prod_1)
    lane = lax.broadcasted_iota(jnp.int32, (LANE, LANE), 1)
    place = lane % 64
    turn = jnp.where(lane < 64, 1.0, -1.0)

    def choose(values, edges):
        out = jnp.full((LANE, LANE), values[-1], jnp.float32)
        for value, edge in zip(values[-2::-1], edges[::-1]):
            out = jnp.where(place < edge, value, out)
        return out

    def phases(t):
        if t < 8:
            bins, edges, signs = CLASSES[t], (20, 40, 60), (1.0, 1.0, -1.0, -1.0)
        else:
            bins, edges, signs = tuple(CLASSES[4 * (t - 8) + i][3] for i in range(4)), (16, 32, 48), (-1.0,) * 4
        angle = [2.0 * math.pi * f / NF for f in bins]
        cosine = choose([SCALE * math.cos(v) for v in angle], edges)
        sine = choose([SCALE * math.sin(v) for v in angle], edges) * turn
        return cosine, sine, choose(signs, edges) * -turn

    def variants(t):
        value = first_ref[:, t * LANE:(t + 1) * LANE].astype(jnp.float32)
        cosine, sine, sign = phases(t)
        turned = pltpu.roll(value, 64, 1)
        one = value * cosine + turned * sine
        return [value * SCALE, one], [turned * (sign * SCALE), pltpu.roll(one, 64, 1) * sign]

    def prepare(c, tail):
        plain, turned = variants(c)
        tail_plain, tail_turned = tail
        here = place // 16 == c % 4
        for lag in range(2):
            if c == 0:
                real = [jnp.where(place < 40, plain[lag], 0.0), jnp.zeros_like(plain[lag])]
                imag = [jnp.where(place < 40, 0.0, plain[lag]), jnp.where(here, tail_plain[lag], 0.0)]
            else:
                real = [plain[lag], jnp.where(here, tail_plain[lag], 0.0)]
                imag = [turned[lag], jnp.where(here, tail_turned[lag], 0.0)]
            for kind, pair in enumerate((real, imag)):
                rows = slice((kind * 2 + lag) * LANE, (kind * 2 + lag + 1) * LANE)
                left[c, rows, :LANE] = pair[0].astype(jnp.bfloat16)
                left[c, rows, LANE:] = pair[1].astype(jnp.bfloat16)

    def multiply(prod, tile, c):
        rows = pl.ds(tile * TILE, TILE)
        if isinstance(c, int):
            main, tail = pl.ds(c * LANE, LANE), pl.ds((8 + c // 4) * LANE, LANE)
        else:
            main = pl.ds(pl.multiple_of(c * LANE, LANE), LANE)
            tail = pl.ds(pl.multiple_of((8 + c // 4) * LANE, LANE), LANE)
        right = jnp.concatenate([all_ref[rows, main], all_ref[rows, tail]], axis=1)
        prod[c] = lax.dot_general(left[c], right, (((1,), (1,)), ((), ())), preferred_element_type=jnp.float32)

    def combine(prod, slot, band, part):
        for block in range(part * BAND // 32, (part + 1) * BAND // 32):
            start = pl.multiple_of(band * BAND + block * 8, 8)
            for lag in range(2):
                for half in range(TILE // WIDE):
                    span = slice(half * WIDE, (half + 1) * WIDE)
                    real = [prod[c, pl.ds(lag * LANE + start, 8), span] for c in range(8)]
                    imag = [prod[c, pl.ds((2 + lag) * LANE + start, 8), span] for c in range(8)]
                    lags = butterflies(real[0], imag[0], real[1:], imag[1:])
                    for m in range(16):
                        outs[slot, lag + 2 * m, pl.ds(start, 8), span] = lags[m]

    def writes(tile, band):
        rows = pl.ds(band * BAND, BAND)
        return pltpu.make_async_copy(
            outs.at[tile % 2, :, rows], out_ref.at[:, rows, pl.ds(tile * TILE, TILE)], sems.at[tile % 2, band]
        )

    bands = LANE // BAND
    tiles = out_ref.shape[2] // TILE
    tails = [variants(8), variants(9)]
    for c in range(8):
        prepare(c, tails[c // 4])
        multiply(prods[0], 0, c)
    for tile in range(tiles):

        for band in range(bands):
            if tile >= 2:
                writes(tile - 2, band).wait()
            for i in range(8 // bands):
                if tile + 1 < tiles:
                    multiply(prods[(tile + 1) % 2], tile + 1, band * (8 // bands) + i)
                combine(prods[tile % 2], tile % 2, band, i)
            writes(tile, band).start()

    for tile in range(max(tiles - 2, 0), tiles):
        for band in range(bands):
            writes(tile, band).wait()


def product_call(first, gathered):
    return pl.pallas_call(
        product_kernel,
        out_shape=jax.ShapeDtypeStruct((NF, 4 * NC, NR * NC), jnp.float32),
        in_specs=[pl.BlockSpec(memory_space=pltpu.VMEM)] * 2,
        out_specs=pl.BlockSpec(memory_space=pl.ANY),
        scratch_shapes=[
            pltpu.VMEM((8, 4 * LANE, 2 * LANE), jnp.bfloat16),
            pltpu.VMEM((8, 4 * LANE, TILE), jnp.float32),
            pltpu.VMEM((8, 4 * LANE, TILE), jnp.float32),
            pltpu.VMEM((2, NF, LANE, TILE), jnp.float32),
            pltpu.SemaphoreType.DMA((2, LANE // BAND)),
        ],
        compiler_params=pltpu.CompilerParams(vmem_limit_bytes=40 * 1024 * 1024),
        name="product",
    )(first, gathered)


def on_device(spectra):
    gathered, first = pl.pallas_call(
        gather_kernel,
        out_shape=(
            jax.ShapeDtypeStruct((NR, NC, DEPTH), jnp.bfloat16),
            jax.ShapeDtypeStruct((4, NC, DEPTH), jnp.bfloat16),
        ),
        in_specs=[pl.BlockSpec(memory_space=pltpu.HBM)],
        out_specs=(pl.BlockSpec(memory_space=pl.ANY), pl.BlockSpec(memory_space=pl.ANY)),
        scratch_shapes=[
            pltpu.VMEM((2, NW, NF, NC), jnp.bfloat16),
            pltpu.VMEM((DEPTH, NC), jnp.float32),
            pltpu.VMEM((DEPTH, NC), jnp.float32),
            pltpu.VMEM((NC, DEPTH), jnp.bfloat16),
            pltpu.SemaphoreType.DMA,
            pltpu.SemaphoreType.DMA((PIECES * NR,)),
            pltpu.SemaphoreType.DMA((3,)),
            pltpu.SemaphoreType.DMA,
            pltpu.SemaphoreType.DMA,
        ],
        compiler_params=pltpu.CompilerParams(
            collective_id=0, has_side_effects=True, vmem_limit_bytes=16 * 1024 * 1024
        ),
        name="gather",
    )(pltpu.with_memory_space_constraint(spectra, pltpu.HBM))
    return product_call(first.reshape(4 * NC, DEPTH), gathered.reshape(NR * NC, DEPTH))


def solution(mesh):
    return jax.shard_map(
        on_device,
        mesh=mesh,
        in_specs=(P(None, None, None, ("col", "row")),),
        out_specs=P(None, "row", "col"),
        check_vma=False,
    )
```

```python
import functools
import math

import jax
import jax.numpy as jnp
from jax import lax
from jax.experimental import pallas as pl
from jax.experimental.pallas import tpu as pltpu
from jax.sharding import PartitionSpec as P

NW, NF, NC, NR = 20, 32, 32, 32
DEPTH = 2 * NW * NF
LANE = 128
SCALE = 1.0 / math.sqrt(float(DEPTH))

PLAN_0 = (
    (5, 0, 0), (4, 1, 0), (1, 0, 0), (2, 0, 0), (0, 0, 0), (3, 0, 0), (2, 1, 0), (5, 1, 0),
    (0, 1, 0), (1, 1, 0), (4, 0, 0), (4, 1, 12), (0, 1, 12), (3, 0, 3), (5, 0, 5), (0, 0, 3),
    (2, 0, 12), (4, 0, 12), (1, 0, 12), (2, 1, 3), (4, 0, 16), (0, 0, 5), (2, 1, 16), (1, 1, 5),
    (3, 1, 5), (3, 0, 16), (1, 0, 5), (1, 0, 1), (2, 1, 12), (0, 1, 1), (4, 1, 1), (3, 1, 3),
    (-1, 0, 4), (3, 0, 5), (0, 1, 5), (4, 1, 8), (2, 1, 8), (2, 1, 28), (4, 0, 15), (-1, 0, 8),
    (1, 0, 13), (-1, 0, 7), (0, 0, 10), (4, 1, 2), (1, 0, 16), (3, 1, 6), (4, 1, 28), (1, 0, 28),
    (2, 0, 28), (0, 1, 9), (3, 1, 16), (4, 0, 28), (-1, 1, 13), (0, 0, 6), (1, 1, 17), (2, 0, 20),
    (-1, 1, 15), (3, 0, 21), (-1, 1, 4), (3, 1, 19), (-1, 0, 2), (-1, 1, 11), (-1, 1, 7), (4, 1, 17),
    (2, 0, 19), (1, 1, 21), (-1, 0, 9), (-1, 0, 11), (-1, 0, 14), (4, 1, 31), (2, 1, 31), (-1, 1, 14),
    (1, 0, 26), (3, 0, 26), (0, 1, 10), (-1, 1, 20), (-1, 0, 24), (-1, 0, 22), (-1, 1, 25), (-1, 0, 31),
    (-1, 0, 29), (-1, 0, 25), (-1, 1, 22), (-1, 1, 18), (-1, 1, 23), (-1, 1, 29), (-1, 0, 17), (-1, 0, 18),
    (-1, 1, 30), (-1, 1, 24), (-1, 1, 27), (-1, 0, 23), (-1, 0, 27), (-1, 0, 30), (-1, 1, 26),
)
PLAN_1 = (
    (5, 1, 0), (2, 1, 0), (3, 1, 0), (6, 1, 0), (4, 0, 0), (5, 0, 0), (1, 0, 0), (0, 0, 0),
    (1, 1, 0), (2, 0, 0), (0, 1, 0), (4, 1, 3), (3, 0, 0), (2, 1, 3), (0, 1, 3), (3, 1, 5),
    (1, 1, 5), (4, 0, 3), (2, 1, 28), (1, 0, 16), (3, 0, 5), (4, 0, 12), (0, 1, 5), (2, 0, 16),
    (1, 0, 1), (3, 1, 3), (1, 0, 5), (3, 1, 4), (4, 1, 15), (2, 1, 15), (-1, 0, 4), (3, 0, 3),
    (4, 1, 1), (1, 1, 28), (2, 0, 15), (0, 1, 9), (2, 1, 19), (3, 0, 16), (4, 0, 15), (3, 1, 6),
    (4, 0, 1), (0, 0, 8), (1, 0, 9), (4, 0, 16), (4, 0, 17), (2, 0, 19), (1, 1, 21), (-1, 1, 2),
    (-1, 1, 7), (0, 1, 11), (2, 1, 21), (1, 1, 16), (-1, 1, 14), (0, 0, 6), (2, 1, 31), (-1, 0, 2),
    (3, 1, 8), (-1, 1, 13), (3, 1, 19), (-1, 0, 14), (4, 0, 19), (3, 0, 19), (2, 1, 25), (-1, 0, 7),
    (0, 0, 11), (1, 0, 24), (0, 0, 10), (1, 0, 20), (-1, 0, 13), (4, 0, 18), (2, 1, 27), (-1, 1, 10),
    (-1, 1, 12), (-1, 1, 30), (-1, 1, 18), (-1, 1, 23), (-1, 1, 17), (-1, 0, 27), (-1, 0, 31), (-1, 1, 20),
    (-1, 1, 24), (-1, 1, 22), (-1, 0, 22), (-1, 0, 29), (-1, 1, 29), (-1, 0, 25), (-1, 0, 28), (-1, 0, 23),
    (-1, 0, 21), (-1, 0, 26), (-1, 0, 30), (-1, 1, 26),
)
PLANS = (PLAN_0, PLAN_1)
PIECES = 2
STEPS = (
    (1, 0, 0), (0, 0, 1), (0, 0, 3), (0, 1, 0), (0, 3, 0), (0, 1, 1), (1, 3, 0),
)
PASS_BEFORE = 14


def ends_of(plan):
    onward = {entry[1:] for entry in plan if entry[0] >= 0}
    every = {(piece, offset) for piece in range(PIECES) for offset in range(NR // 2, NR)}
    return every - onward


def steps_of(plan):
    return sorted({STEPS[entry[0]] for entry in plan if entry[0] >= 0})


def split_offset(offset):
    return offset // 16, offset // 4 % 4, offset % 4


def shifted(offset, step):
    x, z, y = split_offset(offset)
    return (x + step[0]) % 2 * 16 + (z + step[1]) % 4 * 4 + (y + step[2]) % 4


CLASSES = ((0, 16, 8, 24),) + tuple((r, r + 16, 16 - r, 32 - r) for r in range(1, 8))


def gather_kernel(x_ref, all_ref, first_ref, raw, flat, ordered, own, send_sem, recv_sem, first_send, first_recv, local_sem):
    row = lax.axis_index("row")
    col = lax.axis_index("col")
    x, z, y = row // 16, row // 4 % 4, row % 4
    far, core = col // 2, col % 2
    peer = {"row": row, "col": far * 2 + 1 - core}
    target_row = far * 16 + z * 4 + y
    target = {"row": target_row, "col": (1 - far) * 2 + core}
    second = {"row": target_row, "col": far * 2 + core}
    server = {"row": z % 2 * 16 + z * 4 + y, "col": x * 2 + core}
    speaks = core == z // 2
    serves = jnp.logical_and(speaks, x == z % 2)
    keeps = jnp.logical_and(serves, far == x)
    both = jnp.logical_and(serves, far != x)
    passes = jnp.logical_and(speaks, jnp.logical_not(keeps))
    size = NC // PIECES

    back_x = [(x + 2 - i) % 2 for i in range(2)]
    back_z = [(z + 4 - i) % 4 for i in range(4)]
    back_y = [(y + 4 - i) % 4 for i in range(4)]
    part_x, part_z = [v * 16 for v in back_x], [v * 4 for v in back_z]

    def there(step):
        return part_x[-step[0] % 2] + part_z[-step[1] % 4] + back_y[-step[2] % 4]

    def source(offset):
        ox, oz, oy = split_offset(offset)
        return part_x[ox] + part_z[oz] + back_y[oy]

    lines = [back_z[j] == y for j in range(4)]
    serve_line = [jnp.logical_and(serves, v) for v in lines]

    load = pltpu.make_async_copy(x_ref, raw, local_sem)
    load.start()

    barrier = pltpu.get_barrier_semaphore()
    for which, plan in enumerate(PLANS):

        @pl.when(core == which)
        def _():
            for step in steps_of(plan):
                behind = ((-step[0]) % 2, (-step[1]) % 4, (-step[2]) % 4)
                pl.semaphore_signal(barrier, inc=1, device_id={"row": there(behind), "col": col})

    pl.semaphore_signal(barrier, inc=1, device_id=peer)

    @pl.when(passes)
    def _():
        pl.semaphore_signal(barrier, inc=1, device_id=server)

    load.wait()
    flat[:DEPTH, :] = raw[...].reshape(DEPTH, NC).astype(jnp.float32)
    for c, bins in enumerate(CLASSES):
        tail = 8 * LANE + c // 4 * LANE + c % 4 * 16
        for part in range(2):
            for i, f in enumerate(bins):
                start = part * NW * NF + f
                place = c * LANE + part * 64 + i * NW
                if i < 3:
                    ordered[pl.ds(place, NW), :] = flat[pl.ds(start, NW, stride=NF), :]
                else:
                    ordered[pl.ds(place, 4), :] = flat[pl.ds(start, 4, stride=NF), :]
                    ordered[pl.ds(tail + part * 64, 16), :] = flat[pl.ds(start + 4 * NF, 16, stride=NF), :]
    for t in range(10):
        own[:, t * LANE:(t + 1) * LANE] = ordered[t * LANE:(t + 1) * LANE, :].T.astype(jnp.bfloat16)

    keep = pltpu.make_async_copy(own, all_ref.at[row], local_sem)
    keep.start()

    def first_copy(src, dst, which, device):
        return pltpu.make_async_remote_copy(
            src_ref=src, dst_ref=dst, send_sem=first_send.at[which], recv_sem=first_recv, device_id=device
        )

    def all_firsts(sem):
        pltpu.make_async_copy(first_ref, first_ref, sem).wait()

    def serve(piece, offset):
        ox, oz, oy = split_offset(offset)
        rows = pl.ds(piece * size, size)
        src = own.at[rows] if offset == 0 else all_ref.at[source(offset), rows]
        dst = first_ref.at[back_y[oy], rows]

        @pl.when(serve_line[oz])
        def _():
            first_copy(src, dst, 0, target).start()

            @pl.when(both)
            def _():
                first_copy(src, dst, 1, second).start()

            @pl.when(keeps)
            def _():
                first_copy(src, dst, 1, peer).start()
                pltpu.make_async_copy(src, dst, first_recv).start()

    def pass_on():
        @pl.when(passes)
        def _():
            all_firsts(first_recv)
            first_copy(first_ref, first_ref, 2, peer).start()

    def move(plan):
        pl.semaphore_wait(barrier, len(steps_of(plan)) + 1 + jnp.where(both, 2, jnp.where(keeps, 1, 0)))
        late = ends_of(plan)
        seen = set()
        for n, (step, piece, offset) in enumerate(plan):
            if n == len(plan) - PASS_BEFORE:
                pass_on()
            if (piece, offset) in late:
                continue
            rows = pl.ds(piece * size, size)
            place = all_ref.at[source(offset), rows]
            fresh = (piece, offset) not in seen
            seen.add((piece, offset))
            if fresh and offset:
                pltpu.make_async_copy(place, place, recv_sem.at[piece * NR + offset]).wait()
            if step >= 0:
                to = (piece, shifted(offset, STEPS[step]))
                pltpu.make_async_remote_copy(
                    src_ref=own.at[rows] if offset == 0 else place,
                    dst_ref=place,
                    send_sem=send_sem,
                    recv_sem=recv_sem.at[piece * NR + (0 if to in late else to[1])],
                    device_id={"row": there(STEPS[step]), "col": col},
                ).start()
            if fresh and offset < NR // 2:
                serve(piece, offset)
        assert len(seen) + len(late) == PIECES * NR
        for piece in range(PIECES):
            count = sum(1 for entry in late if entry[0] == piece)
            place = all_ref.at[pl.ds(0, count), pl.ds(piece * size, size)]
            pltpu.make_async_copy(place, place, recv_sem.at[piece * NR]).wait()

    for which, plan in enumerate(PLANS):

        @pl.when(core == which)
        def _():
            move(plan)

    @pl.when(jnp.logical_not(passes))
    def _():
        all_firsts(first_recv)

    place = all_ref.at[pl.ds(0, NR - 1)]
    pltpu.make_async_copy(place, place, send_sem).wait()
    keep.wait()

    for which, taken in enumerate((serves, serves, passes)):

        @pl.when(taken)
        def _():
            all_firsts(first_send.at[which])


def butterflies(zero, eight, real, imag):
    c1, c2, c3 = (math.cos(math.pi * k / 8) for k in (1, 2, 3))
    e = [zero] + real + [eight]
    u0, u1, u2, u3, u4 = e[0] + e[8], e[1] + e[7], e[2] + e[6], e[3] + e[5], e[4]
    d0, d1, d2, d3 = e[0] - e[8], e[1] - e[7], e[2] - e[6], e[3] - e[5]
    v0, v1 = u0 + u4, u1 + u3
    w0, w1 = u0 - u4, c2 * (u1 - u3)
    g = c2 * d2
    h0, h1 = d0 + g, d0 - g
    p, q = c1 * d1 + c3 * d3, c3 * d1 - c1 * d3
    v2 = v0 + u2
    even = [v2 + v1, h0 + p, w0 + w1, h1 + q, v0 - u2, h1 - q, w0 - w1, h0 - p, v2 - v1]
    f = [None] + imag
    s1, s2, s3 = f[1] + f[7], f[2] + f[6], f[3] + f[5]
    t1, t2, t3 = f[1] - f[7], f[2] - f[6], f[3] - f[5]
    g = c2 * s2
    a, b = c3 * s1 + c1 * s3, c1 * s1 - c3 * s3
    g0, g1 = g + f[4], g - f[4]
    k = c2 * (t1 + t3)
    odd = [None, a + g0, k + t2, b + g1, t1 - t3, b - g1, k - t2, a - g0]
    out = [even[0]] + [even[m] - odd[m] for m in range(1, 8)] + [even[8]]
    return out + [even[m] + odd[m] for m in range(7, 0, -1)]


TILE = 256
BAND = 64
WIDE = 256


def product_kernel(first_ref, all_ref, out_ref, left, prod_0, prod_1, outs, sems):
    prods = (prod_0, prod_1)
    lane = lax.broadcasted_iota(jnp.int32, (LANE, LANE), 1)
    place = lane % 64
    turn = jnp.where(lane < 64, 1.0, -1.0)

    def choose(values, edges):
        out = jnp.full((LANE, LANE), values[-1], jnp.float32)
        for value, edge in zip(values[-2::-1], edges[::-1]):
            out = jnp.where(place < edge, value, out)
        return out

    def phases(t):
        if t < 8:
            bins, edges, signs = CLASSES[t], (20, 40, 60), (1.0, 1.0, -1.0, -1.0)
        else:
            bins, edges, signs = tuple(CLASSES[4 * (t - 8) + i][3] for i in range(4)), (16, 32, 48), (-1.0,) * 4
        angle = [2.0 * math.pi * f / NF for f in bins]
        cosine = choose([SCALE * math.cos(v) for v in angle], edges)
        sine = choose([SCALE * math.sin(v) for v in angle], edges) * turn
        return cosine, sine, choose(signs, edges) * -turn

    def variants(t):
        value = first_ref[:, t * LANE:(t + 1) * LANE].astype(jnp.float32)
        cosine, sine, sign = phases(t)
        turned = pltpu.roll(value, 64, 1)
        one = value * cosine + turned * sine
        return [value * SCALE, one], [turned * (sign * SCALE), pltpu.roll(one, 64, 1) * sign]

    def prepare(c, tail):
        plain, turned = variants(c)
        tail_plain, tail_turned = tail
        here = place // 16 == c % 4
        for lag in range(2):
            if c == 0:
                real = [jnp.where(place < 40, plain[lag], 0.0), jnp.zeros_like(plain[lag])]
                imag = [jnp.where(place < 40, 0.0, plain[lag]), jnp.where(here, tail_plain[lag], 0.0)]
            else:
                real = [plain[lag], jnp.where(here, tail_plain[lag], 0.0)]
                imag = [turned[lag], jnp.where(here, tail_turned[lag], 0.0)]
            for kind, pair in enumerate((real, imag)):
                rows = slice((kind * 2 + lag) * LANE, (kind * 2 + lag + 1) * LANE)
                left[c, rows, :LANE] = pair[0].astype(jnp.bfloat16)
                left[c, rows, LANE:] = pair[1].astype(jnp.bfloat16)

    def multiply(prod, tile, c):
        rows = pl.ds(tile * TILE, TILE)
        if isinstance(c, int):
            main, tail = pl.ds(c * LANE, LANE), pl.ds((8 + c // 4) * LANE, LANE)
        else:
            main = pl.ds(pl.multiple_of(c * LANE, LANE), LANE)
            tail = pl.ds(pl.multiple_of((8 + c // 4) * LANE, LANE), LANE)
        right = jnp.concatenate([all_ref[rows, main], all_ref[rows, tail]], axis=1)
        prod[c] = lax.dot_general(left[c], right, (((1,), (1,)), ((), ())), preferred_element_type=jnp.float32)

    def combine(prod, slot, band, part):
        for block in range(part * BAND // 32, (part + 1) * BAND // 32):
            start = pl.multiple_of(band * BAND + block * 8, 8)
            for lag in range(2):
                for half in range(TILE // WIDE):
                    span = slice(half * WIDE, (half + 1) * WIDE)
                    real = [prod[c, pl.ds(lag * LANE + start, 8), span] for c in range(8)]
                    imag = [prod[c, pl.ds((2 + lag) * LANE + start, 8), span] for c in range(8)]
                    lags = butterflies(real[0], imag[0], real[1:], imag[1:])
                    for m in range(16):
                        outs[slot, lag + 2 * m, pl.ds(start, 8), span] = lags[m]

    def writes(tile, band):
        rows = pl.ds(band * BAND, BAND)
        return pltpu.make_async_copy(
            outs.at[tile % 2, :, rows], out_ref.at[:, rows, pl.ds(tile * TILE, TILE)], sems.at[tile % 2, band]
        )

    bands = LANE // BAND
    tiles = out_ref.shape[2] // TILE
    tails = [variants(8), variants(9)]
    for c in range(8):
        prepare(c, tails[c // 4])
        multiply(prods[0], 0, c)
    for tile in range(tiles):

        for band in range(bands):
            if tile >= 2:
                writes(tile - 2, band).wait()
            for i in range(8 // bands):
                if tile + 1 < tiles:
                    multiply(prods[(tile + 1) % 2], tile + 1, band * (8 // bands) + i)
                combine(prods[tile % 2], tile % 2, band, i)
            writes(tile, band).start()

    for tile in range(max(tiles - 2, 0), tiles):
        for band in range(bands):
            writes(tile, band).wait()


def product_call(first, gathered):
    return pl.pallas_call(
        product_kernel,
        out_shape=jax.ShapeDtypeStruct((NF, 4 * NC, NR * NC), jnp.float32),
        in_specs=[pl.BlockSpec(memory_space=pltpu.VMEM)] * 2,
        out_specs=pl.BlockSpec(memory_space=pl.ANY),
        scratch_shapes=[
            pltpu.VMEM((8, 4 * LANE, 2 * LANE), jnp.bfloat16),
            pltpu.VMEM((8, 4 * LANE, TILE), jnp.float32),
            pltpu.VMEM((8, 4 * LANE, TILE), jnp.float32),
            pltpu.VMEM((2, NF, LANE, TILE), jnp.float32),
            pltpu.SemaphoreType.DMA((2, LANE // BAND)),
        ],
        compiler_params=pltpu.CompilerParams(vmem_limit_bytes=40 * 1024 * 1024),
        name="product",
    )(first, gathered)


def on_device(spectra):
    gathered, first = pl.pallas_call(
        gather_kernel,
        out_shape=(
            jax.ShapeDtypeStruct((NR, NC, DEPTH), jnp.bfloat16),
            jax.ShapeDtypeStruct((4, NC, DEPTH), jnp.bfloat16),
        ),
        in_specs=[pl.BlockSpec(memory_space=pltpu.HBM)],
        out_specs=(pl.BlockSpec(memory_space=pl.ANY), pl.BlockSpec(memory_space=pl.ANY)),
        scratch_shapes=[
            pltpu.VMEM((2, NW, NF, NC), jnp.bfloat16),
            pltpu.VMEM((DEPTH + 5 * NF, NC), jnp.float32),
            pltpu.VMEM((DEPTH, NC), jnp.float32),
            pltpu.VMEM((NC, DEPTH), jnp.bfloat16),
            pltpu.SemaphoreType.DMA,
            pltpu.SemaphoreType.DMA((PIECES * NR,)),
            pltpu.SemaphoreType.DMA((3,)),
            pltpu.SemaphoreType.DMA,
            pltpu.SemaphoreType.DMA,
        ],
        compiler_params=pltpu.CompilerParams(
            collective_id=0, has_side_effects=True, vmem_limit_bytes=16 * 1024 * 1024
        ),
        name="gather",
    )(pltpu.with_memory_space_constraint(spectra, pltpu.HBM))
    return product_call(first.reshape(4 * NC, DEPTH), gathered.reshape(NR * NC, DEPTH))


def solution(mesh):
    return jax.shard_map(
        on_device,
        mesh=mesh,
        in_specs=(P(None, None, None, ("col", "row")),),
        out_specs=P(None, "row", "col"),
        check_vma=False,
    )
```
